512 devices in a mesh: row: 32 (over z_lo, x), col: 16 (over y, z_hi, core).
Axes of the slice: x: 4, y: 4, z: 16 (z_hi: 2, z_lo: 8; z = z_hi * 8 + z_lo), core: 2. Of those that a mesh axis runs over, the one named last changes fastest.
Arguments:
- queries: bfloat16 [49152, 128], P(('row', 'col')), may hold values from -6 to 6
- key_vectors: bfloat16 [49152, 128], P(('col', 'row')), may hold values from -6 to 6
- value_vectors: bfloat16 [49152, 128], P(('col', 'row')), may hold values from -6 to 6
- outputs: bfloat16 [49152, 128], P(('row', 'col')), may hold values from -3 to 3
- out_grad: bfloat16 [49152, 128], P(('row', 'col')), may hold values from -1.796875 to 1.796875
- logsumexp: float32 [49152], P(('row', 'col')), may hold values from -0.5 to 13
- positions: int32 [49152], P(('row', 'col')), may hold values from 0 to 49151, as said below
Outputs:
- query_grad: bfloat16 [49152, 128], P(('row', 'col'))
- key_grad: bfloat16 [49152, 128], P(('col', 'row'))
- value_grad: bfloat16 [49152, 128], P(('col', 'row'))
The draws below stay inside these ranges and needn't reach their ends.
Inputs may be any that keep to these rules, and one draw needn't show every extreme that they name: positions is a permutation of the token positions; the slots of one device hold position block m and then block 1023 - m, each of 48 consecutive positions in increasing order, for a block number m that differs from device to device.
All inputs are finite; a program needn't handle non-finite values.
Results may differ from the reference program's by a relative error of at most 0.007.
Values may be sent and summed in bfloat16 or wider, within the bound.
A program may use at most 64 MiB of HBM per device.

```python
import math
import jax
import jax.numpy as jnp
from jax import lax

HD = 128
SEQ_DEV = 96
TOKENS = 49152
PAIRS = 512


def paired_slots(key):
    pair_order = jax.random.permutation(key, PAIRS)
    half_block = SEQ_DEV // 2
    offsets = jnp.arange(SEQ_DEV, dtype=jnp.int32)
    early_part = pair_order[:, None] * half_block + offsets[None, :]
    late_part = (2 * PAIRS - 1 - pair_order[:, None]) * half_block + offsets[None, :] - half_block
    slot_grid = jnp.where(offsets[None, :] < half_block, early_part, late_part)
    return slot_grid.reshape(-1).astype(jnp.int32)


def draw_positions(key, part):
    return paired_slots(key)


def draw_logsumexp(key, part):
    slots = paired_slots(key).astype(jnp.float32)
    key = jax.random.fold_in(key, 7)
    jitter = jnp.clip(0.25 * jax.random.normal(key, slots.shape, jnp.float32), -0.75, 0.75)
    offset_base = 0.5
    return (jnp.log(slots + 1.0) + offset_base + jitter).astype(jnp.float32)


def steps_of(own_key, shape, shards, low, largest):
    factor_of = 1.0
    for axis_at, shards_of in shards:
        draws = jax.random.uniform(jax.random.fold_in(jax.random.fold_in(own_key, 6), axis_at), (shards_of,), jnp.float32, low / len(shards), largest / len(shards))
        factor_of = factor_of * jnp.repeat(jnp.exp(draws), shape[axis_at] // shards_of).reshape((-1,) + (1,) * (len(shape) - 1 - axis_at))
    return factor_of


def gaussian(own_key, dims, deviation, bound, split=(), held_as=jnp.bfloat16):
    array = deviation * jax.random.normal(own_key, dims, jnp.float32)
    if split:
        array = array * steps_of(own_key, dims, split, -0.22, 0.18)
    return jnp.clip(array, -bound, bound).astype(held_as)


def setup_inputs(seed: int = 0) -> dict:
    splits = jax.random.split(jax.random.key(seed), 8)
    queries = gaussian(splits[0], (TOKENS, HD), 1.0, 6.0, ((0, 512),))
    key_vectors = gaussian(splits[1], (TOKENS, HD), 1.0, 6.0, ((0, 512),))
    value_vectors = gaussian(splits[2], (TOKENS, HD), 1.0, 6.0, ((0, 512),))
    outputs = gaussian(splits[3], (TOKENS, HD), 0.5, 3.0, ((0, 512),))
    out_grad = gaussian(splits[4], (TOKENS, HD), 0.3, 1.796875, ((0, 512),))
    logsumexp = draw_logsumexp(jax.random.fold_in(splits[7], 71), 0)
    positions = draw_positions(jax.random.fold_in(splits[7], 71), 0)
    return dict(queries=queries, key_vectors=key_vectors, value_vectors=value_vectors, outputs=outputs, out_grad=out_grad, logsumexp=logsumexp, positions=positions)


def block_grads(query_block, dout_block, saved_lse, row_delta, query_pos, key_block, value_block, key_pos):
    scaling = query_block.shape[1] ** -0.5
    scores = jnp.dot(query_block, key_block.T, preferred_element_type=jnp.float32) * scaling
    allowed = key_pos[None, :] <= query_pos[:, None]
    probs_full = jnp.where(allowed, jnp.exp(scores - saved_lse[:, None]), jnp.float32(0.0))
    probs_half = probs_full.astype(jnp.bfloat16)
    dprobs = jnp.dot(dout_block, value_block.T, preferred_element_type=jnp.float32)
    dscores = (scaling * probs_full * (dprobs - row_delta[:, None])).astype(jnp.bfloat16)
    grad_query = jnp.dot(dscores, key_block, preferred_element_type=jnp.float32)
    grad_key = jnp.dot(dscores.T, query_block, preferred_element_type=jnp.float32)
    grad_value = jnp.dot(probs_half.T, dout_block, preferred_element_type=jnp.float32)
    return grad_query, grad_key, grad_value


def reference(queries, key_vectors, value_vectors, outputs, out_grad, logsumexp, positions):
    row_delta = jnp.sum(out_grad.astype(jnp.float32) * outputs.astype(jnp.float32), axis=1)
    block_size = math.gcd(TOKENS, 128)
    block_count = TOKENS // block_size

    def advance(running, inputs_block):
        key_block, value_block, key_pos = inputs_block
        grad_query, grad_key, grad_value = block_grads(queries, out_grad, logsumexp, row_delta, positions, key_block, value_block, key_pos)
        return running + grad_query, (grad_key, grad_value)

    start_value = jnp.zeros((TOKENS, HD), jnp.float32)
    stacked = (key_vectors.reshape(block_count, block_size, HD), value_vectors.reshape(block_count, block_size, HD), positions.reshape(block_count, block_size))
    query_total, (key_parts, value_parts) = lax.scan(advance, start_value, stacked)
    query_grad = query_total.astype(jnp.bfloat16)
    key_grad = key_parts.reshape(TOKENS, HD).astype(jnp.bfloat16)
    value_grad = value_parts.reshape(TOKENS, HD).astype(jnp.bfloat16)
    return (query_grad, key_grad, value_grad)
```

```python
import functools

import jax
import jax.numpy as jnp
from jax import lax
from jax.experimental import pallas as pl
from jax.experimental.pallas import tpu as pltpu
from jax.sharding import PartitionSpec as P

MESH = pl.DeviceIdType.MESH
F32 = jnp.float32
BF16 = jnp.bfloat16
NT = (((1,), (1,)), ((), ()))
NN = (((1,), (0,)), ((), ()))
TN = (((0,), (0,)), ((), ()))
LOG2E = 1.4426950408889634

ROUNDS = ((0, -1, 1, 2), (-2, 3, -3, 4), (-4, 5, -5, 6), (-6, 7, -7, 8))
ROUND_OF = {o: r for r, offs in enumerate(ROUNDS) for o in offs}
PLANE = [(a, b) for a in range(4) for b in range(4) if (a, b) != (0, 0)]


def dot(a, b, dims):
    return lax.dot_general(a, b, dims, preferred_element_type=F32)


def device(x, y, z, core):
    return (lax.rem(z, 8) * 4 + x, (y * 2 + z // 8) * 2 + core)


def kernel(
    half, q_ref, k_ref, v_ref, o_ref, do_ref, lse_ref, pos_ref,
    gq_ref, gk_ref, gv_ref,
    qbuf, kbuf, rowbuf, mrow, mbuf, pk, rows, dq, dk, dv,
    sib_out, sib_in, dq_out, dq_in, kv_out, kv_in,
    send_sem, q_recv, qs_recv, k_recv, m_recv, mb_recv, sib_recv, dq_recv, kv_recv,
):
    width = q_ref.shape[1]
    shard = 2 * half
    scale = width ** -0.5
    row, col = lax.axis_index("row"), lax.axis_index("col")
    z_lo, x = row // 4, lax.rem(row, 4)
    core, z_hi, y = lax.rem(col, 2), lax.rem(col // 2, 2), col // 4
    z = z_hi * 8 + z_lo
    other = 1 - core

    def at_z(o):
        return device(x, y, lax.rem(z + o + 16, 16), core)

    def at_plane(a, b):
        return device(lax.rem(x + a, 4), lax.rem(y + b, 4), z, core)

    sibling = device(x, y, z, other)

    to_z = lax.rem(z, 2) * 8 + lax.rem(x, 2) * 4 + y
    to_core = x // 2
    to_self = jnp.logical_and(to_z == z, to_core == core)
    my_mslot = (z_hi * 2 + core) * 4 + z_lo // 2
    collects = jnp.logical_and(x == core * 2 + z_lo // 4, y == lax.rem(z_lo, 4))

    def holder(slot):
        xo, yo = slot // 4, slot % 4
        hz, hc = (xo // 2) * 8 + 2 * yo + z_hi, xo % 2
        return hz, hc, jnp.logical_and(hz == z, hc == core)

    barrier = pltpu.get_barrier_semaphore()
    for o in range(1, 16):
        pl.semaphore_signal(barrier, inc=1, device_id=at_z(o), device_id_type=MESH)
    for a, b in PLANE:
        pl.semaphore_signal(barrier, inc=1, device_id=at_plane(a, b), device_id_type=MESH)
    pl.semaphore_signal(barrier, inc=1, device_id=sibling, device_id_type=MESH)
    for slot in range(16):
        hz, hc, mine = holder(slot)

        @pl.when(jnp.logical_and(collects, jnp.logical_not(mine)))
        def _():
            pl.semaphore_signal(
                barrier, inc=1, device_id=device(x, y, hz, hc), device_id_type=MESH
            )

    sends = []

    def send(src, dst, recv_sem, target):
        cp = pltpu.make_async_remote_copy(
            src_ref=src, dst_ref=dst, send_sem=send_sem.at[len(sends)], recv_sem=recv_sem,
            device_id=target, device_id_type=MESH,
        )
        sends.append(cp)
        cp.start()

    def arrived(dst, recv_sem):
        pltpu.make_async_remote_copy(
            src_ref=dst, dst_ref=dst, send_sem=send_sem.at[0], recv_sem=recv_sem,
            device_id=sibling, device_id_type=MESH,
        ).wait_recv()

    my_qslot = lax.rem(z, 4) * 2 + core
    my_kslot = x * 4 + y
    qbuf[0, my_qslot, 0:shard] = q_ref[...]
    qbuf[0, my_qslot, shard:2 * shard] = do_ref[...]
    kbuf[my_kslot, 0:shard] = k_ref[...]
    kbuf[my_kslot, shard:2 * shard] = v_ref[...]
    prod = do_ref[...].astype(F32) * o_ref[...].astype(F32)
    rowbuf[...] = jnp.zeros_like(rowbuf)
    rowbuf[0:1, 0:shard] = lse_ref[...] * LOG2E
    rowbuf[1:2, 0:shard] = jnp.sum(prod.T, axis=0, keepdims=True)
    base = jnp.broadcast_to(pos_ref[0:1, 0:1].astype(F32), (1, 128))
    mrow[...] = base
    shift = lax.rem(my_qslot * half, 128)
    early = pltpu.roll(rowbuf[...], shift, 1)
    late = pltpu.roll(rowbuf[...], lax.rem(shift + 128 - half, 128), 1)
    sub = lax.broadcasted_iota(jnp.int32, (8, 128), 0)
    full = jnp.where(
        sub < 2, early,
        jnp.where(sub < 4, pltpu.roll(late, 2, 0), jnp.where(sub == 4, jnp.broadcast_to(base, (8, 128)), 0.0)),
    )
    hi = full.astype(BF16).astype(F32)
    mid = (full - hi).astype(BF16).astype(F32)
    low = full - hi - mid
    parts = jnp.concatenate([hi, mid, low, jnp.zeros_like(hi)], axis=0)
    qbuf[0, my_qslot, 2 * shard:2 * shard + 32] = parts.astype(BF16)

    pl.semaphore_wait(barrier, 31 + jnp.where(to_self, 0, 1))

    def qslot(o):
        return lax.rem(z + o + 16, 4) * 2 + core

    def sslot(o):
        return lax.rem(z + o + 16, 4) * 2 + other

    def relay(o):
        src = qbuf.at[ROUND_OF[o], qslot(o)]
        for sign in ((1, -1) if o == 0 else ((1,) if o < 0 else (-1,))):
            for d in (2, 1):
                there = o - sign * d
                if there in ROUND_OF and abs(there) <= 8:
                    send(src, qbuf.at[ROUND_OF[there], qslot(o)], q_recv.at[there + 7], at_z(sign * d))

    def to_sibling(o):
        ref = qbuf.at[ROUND_OF[o], qslot(o)]
        send(ref, ref, qs_recv.at[o + 7], sibling)

    def take(o):
        arrived(qbuf.at[ROUND_OF[o], qslot(o)], q_recv.at[o + 7])

    relay(0)
    to_sibling(0)
    for i, (a, b) in enumerate(PLANE):
        ref = kbuf.at[my_kslot]
        send(ref, ref, k_recv.at[i], at_plane(a, b))

    m_copy = pltpu.make_async_remote_copy(
        src_ref=mrow, dst_ref=mbuf.at[my_mslot], send_sem=send_sem.at[send_sem.shape[0] - 1],
        recv_sem=m_recv.at[my_mslot], device_id=device(x, y, to_z, to_core), device_id_type=MESH,
    )

    @pl.when(jnp.logical_not(to_self))
    def _():
        m_copy.start()

    @pl.when(to_self)
    def _():
        mbuf[my_mslot] = mrow[...]

    lane = lax.broadcasted_iota(jnp.int32, (8, 128), 1)

    def unpack(r):
        tiles = []
        pieces = []
        for s in range(8):
            raw = qbuf[r, s, 2 * shard:2 * shard + 32].astype(F32)
            pieces.append(raw[0:8] + raw[8:16] + raw[16:24])
        for j in range(8 * half // 128):
            first, last = 128 * j // half, (128 * j + 127) // half
            tile = pieces[last]
            for s in range(last - 1, first - 1, -1):
                tile = jnp.where(lane < (s + 1) * half - 128 * j, pieces[s], tile)
            tiles.append(tile)
        rows[r] = jnp.concatenate(tiles, axis=1)

    nq = 8 * half
    nk = 8 * half
    lanes = lax.broadcasted_iota(jnp.int32, (1, nq), 1).astype(F32)
    offs = lanes - half * jnp.floor((lanes + 0.5) * (1.0 / half))
    top = 1023.0 * half

    def block(r, kh, qh, kb, masked, first_q, first_k):
        k = kbuf[8 * kb:8 * kb + 8, kh * half:(kh + 1) * half].reshape(nk, width)
        v = kbuf[8 * kb:8 * kb + 8, shard + kh * half:shard + (kh + 1) * half].reshape(nk, width)
        q = qbuf[r, :, qh * half:(qh + 1) * half].reshape(nq, width)
        do = qbuf[r, :, shard + qh * half:shard + (qh + 1) * half].reshape(nq, width)
        lse = rows[r, 2 * qh:2 * qh + 1]
        delta = rows[r, 2 * qh + 1:2 * qh + 2]
        s = dot(k, q, NT)
        dp = dot(v, do, NT)
        p = jnp.exp2(s * (scale * LOG2E) - lse)
        if masked:
            start = rows[r, 4:5]
            pq = (start if qh == 0 else top - start) + offs
            pkk = jnp.concatenate([pk[kh, nk * kb:nk * (kb + 1)]] * (nq // 128), axis=1)
            p = jnp.where(pkk <= pq, p, 0.0)
        ds = (p * (dp - delta)).astype(BF16)
        ph = p.astype(BF16)
        gv, gk, gq = dot(ph, do, NN), dot(ds, q, NN), dot(ds, k, TN)
        span = slice(nk * kb, nk * (kb + 1))
        if first_k:
            dv[kh, span] = gv
            dk[kh, span] = gk
        else:
            dv[kh, span] += gv
            dk[kh, span] += gk
        gq = gq.reshape(8, half, width)
        if first_q:
            dq[r, qh] = gq
        else:
            dq[r, qh] += gq

    def late_early(r, first):
        for kb in range(2):
            block(r, 0, 1, kb, False, kb == 0, first)

    def diagonal(r, first):
        for kb in range(2):
            block(r, 0, 0, kb, True, kb == 0, False)
        for kb in range(2):
            block(r, 1, 1, kb, True, False, first)

    def ready(r):
        for o in ROUNDS[r]:
            arrived(qbuf.at[r, sslot(o)], qs_recv.at[o + 7])
        unpack(r)

    def stage(k):
        for o in (-2 * k, 2 * k):
            if o in ROUND_OF:
                take(o)
                if k < 4:
                    relay(o)
                to_sibling(o)
        for o in (-2 * k + 1, 2 * k - 1):
            take(o)
            to_sibling(o)

    stage(1)
    ready(0)
    for i, (a, b) in enumerate(PLANE):
        arrived(kbuf.at[lax.rem(x - a + 4, 4) * 4 + lax.rem(y - b + 4, 4)], k_recv.at[i])
    late_early(0, True)
    stage(2)

    for slot in range(16):
        hz, hc, mine = holder(slot)

        @pl.when(jnp.logical_and(collects, jnp.logical_not(mine)))
        def _():
            arrived(mbuf.at[slot], m_recv.at[slot])

    mb_copies = [
        pltpu.make_async_remote_copy(
            src_ref=mbuf, dst_ref=mbuf, send_sem=send_sem.at[send_sem.shape[0] - 2 - i],
            recv_sem=mb_recv.at[0], device_id=at_plane(a, b), device_id_type=MESH,
        )
        for i, (a, b) in enumerate(PLANE)
    ]

    @pl.when(collects)
    def _():
        for cp in mb_copies:
            cp.start()

    ready(1)
    late_early(1, False)
    stage(3)
    ready(2)
    late_early(2, False)
    stage(4)
    ready(3)
    late_early(3, False)

    @pl.when(jnp.logical_not(collects))
    def _():
        arrived(mbuf, mb_recv.at[0])

    sub48 = lax.broadcasted_iota(jnp.int32, (half, 128), 0).astype(F32)
    for slot in range(16):
        start = jnp.broadcast_to(mbuf[slot], (half, 128))
        pk[0, slot * half:(slot + 1) * half] = start + sub48
        pk[1, slot * half:(slot + 1) * half] = top - start + sub48

    def share(r):
        for i, o in enumerate(ROUNDS[r]):
            sib_out[r, i, 0:half] = dq[r, 0, sslot(o)].astype(BF16)
            sib_out[r, i, half:shard] = dq[r, 1, sslot(o)].astype(BF16)
        send(sib_out.at[r], sib_in.at[r], sib_recv.at[r], sibling)

    def home(r):
        arrived(sib_in.at[r], sib_recv.at[r])
        for i, o in enumerate(ROUNDS[r]):
            for h in range(2):
                span = slice(h * half, (h + 1) * half)
                total = dq[r, h, qslot(o)] + sib_in[r, i, span].astype(F32)
                if o == 0:
                    dq[r, h, qslot(o)] = total
                else:
                    dq_out[r, i, span] = total.astype(BF16)
            if o != 0:
                send(dq_out.at[r, i], dq_in.at[o + 7], dq_recv.at[o + 7], at_z(o))

    diagonal(3, True)
    share(3)
    diagonal(2, False)
    share(2)
    home(3)
    diagonal(1, False)
    share(1)
    home(2)
    diagonal(0, False)
    share(0)
    home(1)

    for i, (a, b) in enumerate(PLANE):
        slot = lax.rem(x + a, 4) * 4 + lax.rem(y + b, 4)
        for h in range(2):
            span = pl.ds(pl.multiple_of(slot * half, 16), half)
            kv_out[i, 0, h * half:(h + 1) * half] = dk[h, span].astype(BF16)
            kv_out[i, 1, h * half:(h + 1) * half] = dv[h, span].astype(BF16)
        send(kv_out.at[i], kv_in.at[i], kv_recv.at[i], at_plane(a, b))
    home(0)

    totals = []
    for h in range(2):
        totals.append(dq[0, h, my_qslot])
    for r in (0, 1, 2, 3):
        for o in ROUNDS[r]:
            if o != 0:
                arrived(dq_in.at[o + 7], dq_recv.at[o + 7])
                for h in range(2):
                    totals[h] = totals[h] + dq_in[o + 7, h * half:(h + 1) * half].astype(F32)
    for h in range(2):
        gq_ref[h * half:(h + 1) * half] = (totals[h] * scale).astype(BF16)

    for i in range(15):
        arrived(kv_in.at[i], kv_recv.at[i])
    for h in range(2):
        span = pl.ds(pl.multiple_of(my_kslot * half, 16), half)
        rowspan = slice(h * half, (h + 1) * half)
        sk, sv = dk[h, span], dv[h, span]
        for i in range(15):
            sk = sk + kv_in[i, 0, rowspan].astype(F32)
            sv = sv + kv_in[i, 1, rowspan].astype(F32)
        gk_ref[rowspan] = (sk * scale).astype(BF16)
        gv_ref[rowspan] = sv.astype(BF16)

    for cp in sends:
        cp.wait_send()

    @pl.when(jnp.logical_not(to_self))
    def _():
        m_copy.wait_send()

    @pl.when(collects)
    def _():
        for cp in mb_copies:
            cp.wait_send()


def shards(queries, key_vectors, value_vectors, outputs, out_grad, logsumexp, positions):
    shard, width = queries.shape
    half = shard // 2
    vmem = pl.BlockSpec(memory_space=pltpu.VMEM)
    dma = pltpu.SemaphoreType.DMA
    return pl.pallas_call(
        functools.partial(kernel, half),
        name="attention_backward",
        out_shape=[jax.ShapeDtypeStruct((shard, width), BF16)] * 3,
        in_specs=[vmem] * 7,
        out_specs=[vmem] * 3,
        scratch_shapes=[
            pltpu.VMEM((4, 8, 2 * shard + 32, width), BF16),
            pltpu.VMEM((16, 2 * shard, width), BF16),
            pltpu.VMEM((8, 128), F32),
            pltpu.VMEM((1, 128), F32),
            pltpu.VMEM((16, 1, 128), F32),
            pltpu.VMEM((2, 16 * half, 128), F32),
            pltpu.VMEM((4, 8, 8 * half), F32),
            pltpu.VMEM((4, 2, 8, half, width), F32),
            pltpu.VMEM((2, 16 * half, width), F32),
            pltpu.VMEM((2, 16 * half, width), F32),
            pltpu.VMEM((4, 4, shard, width), BF16),
            pltpu.VMEM((4, 4, shard, width), BF16),
            pltpu.VMEM((4, 4, shard, width), BF16),
            pltpu.VMEM((16, shard, width), BF16),
            pltpu.VMEM((15, 2, shard, width), BF16),
            pltpu.VMEM((15, 2, shard, width), BF16),
            dma((128,)),
            dma((16,)),
            dma((16,)),
            dma((15,)),
            dma((16,)),
            dma((1,)),
            dma((4,)),
            dma((16,)),
            dma((15,)),
        ],
        compiler_params=pltpu.CompilerParams(
            collective_id=0, has_side_effects=True, vmem_limit_bytes=48 * 2 ** 20
        ),
    )(
        queries, key_vectors, value_vectors, outputs, out_grad,
        logsumexp.reshape(1, shard), positions.reshape(1, shard),
    )


def solution(mesh):
    in_specs = (
        P(("row", "col"), None),
        P(("col", "row"), None),
        P(("col", "row"), None),
        P(("row", "col"), None),
        P(("row", "col"), None),
        P(("row", "col")),
        P(("row", "col")),
    )
    out_specs = (P(("row", "col"), None), P(("col", "row"), None), P(("col", "row"), None))
    return jax.shard_map(shards, mesh=mesh, in_specs=in_specs, out_specs=out_specs, check_vma=False)
```

```python
import functools

import jax
import jax.numpy as jnp
from jax import lax
from jax.experimental import pallas as pl
from jax.experimental.pallas import tpu as pltpu
from jax.sharding import PartitionSpec as P

MESH = pl.DeviceIdType.MESH
F32 = jnp.float32
BF16 = jnp.bfloat16
NT = (((1,), (1,)), ((), ()))
NN = (((1,), (0,)), ((), ()))
TN = (((0,), (0,)), ((), ()))
LOG2E = 1.4426950408889634

ROUNDS = ((0, -1, 1, 2), (-2, 3, -3, 4), (-4, 5, -5, 6), (-6, 7, -7, 8))
ROUND_OF = {o: r for r, offs in enumerate(ROUNDS) for o in offs}
HAND_ON = {8: 7, -7: -6, 6: 5, -5: -4, 4: 3, -3: -2, 2: 1}
TAKES = {b: a for a, b in HAND_ON.items()}
FINAL = tuple(o for offs in ROUNDS for o in offs if o != 0 and o not in HAND_ON)
PLANE = [(a, b) for a in range(4) for b in range(4) if (a, b) != (0, 0)]


def dot(a, b, dims):
    return lax.dot_general(a, b, dims, preferred_element_type=F32)


def device(x, y, z, core):
    return (lax.rem(z, 8) * 4 + x, (y * 2 + z // 8) * 2 + core)


def kernel(
    half, q_hbm, k_hbm, v_hbm, o_hbm, do_hbm, lse_hbm, pos_hbm,
    gq_ref, gk_ref, gv_ref,
    qbuf, kbuf, o_ref, lse_ref, pos_ref, rowbuf, mrow, mbuf, pk, rows, dq, dk, dv,
    sib_out, sib_in, dq_out, pair_in, dq_in, kv_out, kv_in,
    in_sem, send_sem, q_recv, qs_recv, k_recv, m_recv, mb_recv, sib_recv, pair_recv, dq_recv, kv_recv,
):
    width = q_hbm.shape[1]
    shard = 2 * half
    scale = width ** -0.5
    row, col = lax.axis_index("row"), lax.axis_index("col")
    z_lo, x = row // 4, lax.rem(row, 4)
    core, z_hi, y = lax.rem(col, 2), lax.rem(col // 2, 2), col // 4
    z = z_hi * 8 + z_lo
    other = 1 - core

    def at_z(o):
        return device(x, y, lax.rem(z + o + 16, 16), core)

    def at_plane(a, b):
        return device(lax.rem(x + a, 4), lax.rem(y + b, 4), z, core)

    sibling = device(x, y, z, other)

    to_z = lax.rem(z, 2) * 8 + lax.rem(x, 2) * 4 + y
    to_core = x // 2
    to_self = jnp.logical_and(to_z == z, to_core == core)
    my_mslot = (z_hi * 2 + core) * 4 + z_lo // 2
    collects = jnp.logical_and(x == core * 2 + z_lo // 4, y == lax.rem(z_lo, 4))

    def holder(slot):
        xo, yo = slot // 4, slot % 4
        hz, hc = (xo // 2) * 8 + 2 * yo + z_hi, xo % 2
        return hz, hc, jnp.logical_and(hz == z, hc == core)

    my_qslot = lax.rem(z, 4) * 2 + core
    my_kslot = x * 4 + y
    inputs = [
        pltpu.make_async_copy(src, dst, in_sem.at[i])
        for i, (src, dst) in enumerate((
            (do_hbm, qbuf.at[0, my_qslot, pl.ds(shard, shard)]),
            (o_hbm, o_ref),
            (lse_hbm, lse_ref),
            (pos_hbm, pos_ref),
            (q_hbm, qbuf.at[0, my_qslot, pl.ds(0, shard)]),
            (k_hbm, kbuf.at[my_kslot, pl.ds(0, shard)]),
            (v_hbm, kbuf.at[my_kslot, pl.ds(shard, shard)]),
        ))
    ]
    for cp in inputs:
        cp.start()

    barrier = pltpu.get_barrier_semaphore()
    for o in range(1, 16):
        pl.semaphore_signal(barrier, inc=1, device_id=at_z(o), device_id_type=MESH)
    for a, b in PLANE:
        pl.semaphore_signal(barrier, inc=1, device_id=at_plane(a, b), device_id_type=MESH)
    pl.semaphore_signal(barrier, inc=1, device_id=sibling, device_id_type=MESH)
    for slot in range(16):
        hz, hc, mine = holder(slot)

        @pl.when(jnp.logical_and(collects, jnp.logical_not(mine)))
        def _():
            pl.semaphore_signal(
                barrier, inc=1, device_id=device(x, y, hz, hc), device_id_type=MESH
            )

    sends = []

    def send(src, dst, recv_sem, target):
        cp = pltpu.make_async_remote_copy(
            src_ref=src, dst_ref=dst, send_sem=send_sem.at[len(sends)], recv_sem=recv_sem,
            device_id=target, device_id_type=MESH,
        )
        sends.append(cp)
        cp.start()

    def arrived(dst, recv_sem):
        pltpu.make_async_remote_copy(
            src_ref=dst, dst_ref=dst, send_sem=send_sem.at[0], recv_sem=recv_sem,
            device_id=sibling, device_id_type=MESH,
        ).wait_recv()

    for cp in inputs:
        cp.wait()
    prod = qbuf[0, my_qslot, shard:2 * shard].astype(F32) * o_ref[...].astype(F32)
    rowbuf[...] = jnp.zeros_like(rowbuf)
    rowbuf[0:1, 0:shard] = lse_ref[...] * LOG2E
    rowbuf[1:2, 0:shard] = jnp.sum(prod.T, axis=0, keepdims=True)
    base = jnp.broadcast_to(pos_ref[0:1, 0:1].astype(F32), (1, 128))
    mrow[...] = base
    shift = lax.rem(my_qslot * half, 128)
    early = pltpu.roll(rowbuf[...], shift, 1)
    late = pltpu.roll(rowbuf[...], lax.rem(shift + 128 - half, 128), 1)
    sub = lax.broadcasted_iota(jnp.int32, (8, 128), 0)
    full = jnp.where(
        sub < 2, early,
        jnp.where(sub < 4, pltpu.roll(late, 2, 0), jnp.where(sub == 4, jnp.broadcast_to(base, (8, 128)), 0.0)),
    )
    hi = full.astype(BF16).astype(F32)
    mid = (full - hi).astype(BF16).astype(F32)
    qbuf[0, my_qslot, 2 * shard:2 * shard + 16] = jnp.concatenate([hi, mid], axis=0).astype(BF16)

    pl.semaphore_wait(barrier, 31 + jnp.where(to_self, 0, 1))

    def qslot(o):
        return lax.rem(z + o + 16, 4) * 2 + core

    def sslot(o):
        return lax.rem(z + o + 16, 4) * 2 + other

    chunks = (pl.ds(0, shard), pl.ds(shard, shard + 16))

    def directions(o):
        return (1, -1) if o == 0 else ((1,) if o < 0 else (-1,))

    def relay(o, c):
        for sign in directions(o):
            there = o - sign * 2
            if there in ROUND_OF:
                send(
                    qbuf.at[ROUND_OF[o], qslot(o), chunks[c]],
                    qbuf.at[ROUND_OF[there], qslot(o), chunks[c]],
                    q_recv.at[c, there + 7], at_z(sign * 2),
                )

    def deliver(o):
        for sign in directions(o):
            there = o - sign
            send(
                qbuf.at[ROUND_OF[o], qslot(o)], qbuf.at[ROUND_OF[there], qslot(o)],
                q_recv.at[1, there + 7], at_z(sign),
            )

    def to_sibling(o):
        ref = qbuf.at[ROUND_OF[o], qslot(o)]
        send(ref, ref, qs_recv.at[o + 7], sibling)

    def take(o, c):
        arrived(qbuf.at[ROUND_OF[o], qslot(o), chunks[c]], q_recv.at[c, o + 7])

    def take_whole(o):
        arrived(qbuf.at[ROUND_OF[o], qslot(o)], q_recv.at[1, o + 7])

    relay(0, 0)
    relay(0, 1)
    deliver(0)
    to_sibling(0)
    for i, (a, b) in enumerate(PLANE):
        ref = kbuf.at[my_kslot]
        send(ref, ref, k_recv.at[i], at_plane(a, b))

    m_copy = pltpu.make_async_remote_copy(
        src_ref=mrow, dst_ref=mbuf.at[my_mslot], send_sem=send_sem.at[send_sem.shape[0] - 1],
        recv_sem=m_recv.at[my_mslot], device_id=device(x, y, to_z, to_core), device_id_type=MESH,
    )

    @pl.when(jnp.logical_not(to_self))
    def _():
        m_copy.start()

    @pl.when(to_self)
    def _():
        mbuf[my_mslot] = mrow[...]

    lane = lax.broadcasted_iota(jnp.int32, (8, 128), 1)

    def unpack(r):
        tiles = []
        pieces = []
        for s in range(8):
            raw = qbuf[r, s, 2 * shard:2 * shard + 16].astype(F32)
            pieces.append(raw[0:8] + raw[8:16])
        for j in range(8 * half // 128):
            first, last = 128 * j // half, (128 * j + 127) // half
            tile = pieces[last]
            for s in range(last - 1, first - 1, -1):
                tile = jnp.where(lane < (s + 1) * half - 128 * j, pieces[s], tile)
            tiles.append(tile)
        rows[r] = jnp.concatenate(tiles, axis=1)

    nq = 8 * half
    nk = 8 * half
    lanes = lax.broadcasted_iota(jnp.int32, (1, nq), 1).astype(F32)
    offs = lanes - half * jnp.floor((lanes + 0.5) * (1.0 / half))
    top = 1023.0 * half

    def block(r, kh, qh, kb, masked, first_q, first_k):
        k = kbuf[8 * kb:8 * kb + 8, kh * half:(kh + 1) * half].reshape(nk, width)
        v = kbuf[8 * kb:8 * kb + 8, shard + kh * half:shard + (kh + 1) * half].reshape(nk, width)
        q = qbuf[r, :, qh * half:(qh + 1) * half].reshape(nq, width)
        do = qbuf[r, :, shard + qh * half:shard + (qh + 1) * half].reshape(nq, width)
        lse = rows[r, 2 * qh:2 * qh + 1]
        delta = rows[r, 2 * qh + 1:2 * qh + 2]
        s = dot(k, q, NT)
        dp = dot(v, do, NT)
        p = jnp.exp2(s * (scale * LOG2E) - lse)
        if masked:
            start = rows[r, 4:5]
            pq = (start if qh == 0 else top - start) + offs
            pkk = jnp.concatenate([pk[kh, nk * kb:nk * (kb + 1)]] * (nq // 128), axis=1)
            p = jnp.where(pkk <= pq, p, 0.0)
        ds = (p * (dp - delta)).astype(BF16)
        ph = p.astype(BF16)
        gv, gk, gq = dot(ph, do, NN), dot(ds, q, NN), dot(ds, k, TN)
        span = slice(nk * kb, nk * (kb + 1))
        if first_k:
            dv[kh, span] = gv
            dk[kh, span] = gk
        else:
            dv[kh, span] += gv
            dk[kh, span] += gk
        gq = gq.reshape(8, half, width)
        if first_q:
            dq[r, qh] = gq
        else:
            dq[r, qh] += gq

    def late_early(r, first):
        for kb in range(2):
            block(r, 0, 1, kb, False, kb == 0, first)

    def early_early(r):
        for kb in range(2):
            block(r, 0, 0, kb, True, kb == 0, False)

    def late_late(r, first):
        for kb in range(2):
            block(r, 1, 1, kb, True, False, first)

    def ready(r):
        for o in ROUNDS[r]:
            arrived(qbuf.at[r, sslot(o)], qs_recv.at[o + 7])
        unpack(r)

    def stage(k):
        far = [o for o in (-2 * k, 2 * k) if o in ROUND_OF]
        for c in range(2):
            for o in far:
                take(o, c)
                if k < 4:
                    relay(o, c)
        for o in far:
            if k < 4:
                deliver(o)
            to_sibling(o)
        for o in (-2 * k + 1, 2 * k - 1):
            take_whole(o)
            to_sibling(o)

    def share(r):
        for i, o in enumerate(ROUNDS[r]):
            sib_out[r, i, 0:half] = dq[r, 0, sslot(o)].astype(BF16)
            sib_out[r, i, half:shard] = dq[r, 1, sslot(o)].astype(BF16)
        send(sib_out.at[r], sib_in.at[r], sib_recv.at[r], sibling)

    def home_far(r):
        arrived(sib_in.at[r], sib_recv.at[r])
        for i, o in enumerate(ROUNDS[r]):
            if o in HAND_ON or o == -1:
                for h in range(2):
                    span = slice(h * half, (h + 1) * half)
                    dq_out[r, i, span] = (dq[r, h, qslot(o)] + sib_in[r, i, span].astype(F32)).astype(BF16)
                if o == -1:
                    send(dq_out.at[r, i], dq_in.at[FINAL.index(o)], dq_recv.at[FINAL.index(o)], at_z(o))
                else:
                    there = HAND_ON[o]
                    j = ROUNDS[r].index(there)
                    send(dq_out.at[r, i], pair_in.at[r, j], pair_recv.at[r, j], at_z(o - there))

    def home_near(r):
        for i, o in enumerate(ROUNDS[r]):
            if o in TAKES or o == 0:
                if o != 0:
                    arrived(pair_in.at[r, i], pair_recv.at[r, i])
                for h in range(2):
                    span = slice(h * half, (h + 1) * half)
                    total = dq[r, h, qslot(o)] + sib_in[r, i, span].astype(F32)
                    if o == 0:
                        dq[r, h, qslot(o)] = total
                    else:
                        dq_out[r, i, span] = (total + pair_in[r, i, span].astype(F32)).astype(BF16)
                if o != 0:
                    send(dq_out.at[r, i], dq_in.at[FINAL.index(o)], dq_recv.at[FINAL.index(o)], at_z(o))

    def keys_home(h):
        for i, (a, b) in enumerate(PLANE):
            slot = lax.rem(x + a, 4) * 4 + lax.rem(y + b, 4)
            span = pl.ds(pl.multiple_of(slot * half, 16), half)
            kv_out[i, h, 0] = dk[h, span].astype(BF16)
            kv_out[i, h, 1] = dv[h, span].astype(BF16)
            send(kv_out.at[i, h], kv_in.at[i, h], kv_recv.at[i, h], at_plane(a, b))

    stage(1)
    ready(0)
    for i, (a, b) in enumerate(PLANE):
        arrived(kbuf.at[lax.rem(x - a + 4, 4) * 4 + lax.rem(y - b + 4, 4)], k_recv.at[i])
    late_early(0, True)
    stage(2)

    for slot in range(16):
        hz, hc, mine = holder(slot)

        @pl.when(jnp.logical_and(collects, jnp.logical_not(mine)))
        def _():
            arrived(mbuf.at[slot], m_recv.at[slot])

    mb_copies = [
        pltpu.make_async_remote_copy(
            src_ref=mbuf, dst_ref=mbuf, send_sem=send_sem.at[send_sem.shape[0] - 2 - i],
            recv_sem=mb_recv.at[0], device_id=at_plane(a, b), device_id_type=MESH,
        )
        for i, (a, b) in enumerate(PLANE)
    ]

    @pl.when(collects)
    def _():
        for cp in mb_copies:
            cp.start()

    ready(1)
    late_early(1, False)
    stage(3)
    ready(2)
    late_early(2, False)

    @pl.when(jnp.logical_not(collects))
    def _():
        arrived(mbuf, mb_recv.at[0])

    sub48 = lax.broadcasted_iota(jnp.int32, (half, 128), 0).astype(F32)
    for slot in range(16):
        start = jnp.broadcast_to(mbuf[slot], (half, 128))
        pk[0, slot * half:(slot + 1) * half] = start + sub48
        pk[1, slot * half:(slot + 1) * half] = top - start + sub48

    early_early(0)
    late_late(0, True)
    share(0)
    early_early(1)
    late_late(1, False)
    share(1)
    home_far(0)
    stage(4)
    home_near(0)
    home_far(1)
    ready(3)
    late_early(3, False)
    early_early(3)
    late_late(3, False)
    share(3)
    home_near(1)
    early_early(2)
    keys_home(0)
    home_far(3)
    late_late(2, False)
    share(2)
    keys_home(1)
    home_near(3)
    home_far(2)
    home_near(2)

    for h in range(2):
        span = pl.ds(pl.multiple_of(my_kslot * half, 16), half)
        rowspan = slice(h * half, (h + 1) * half)
        sk, sv = dk[h, span], dv[h, span]
        for i in range(15):
            arrived(kv_in.at[i, h], kv_recv.at[i, h])
            sk = sk + kv_in[i, h, 0].astype(F32)
            sv = sv + kv_in[i, h, 1].astype(F32)
        gk_ref[rowspan] = (sk * scale).astype(BF16)
        gv_ref[rowspan] = sv.astype(BF16)

    totals = [dq[0, h, my_qslot] for h in range(2)]
    for i in range(len(FINAL)):
        arrived(dq_in.at[i], dq_recv.at[i])
        for h in range(2):
            totals[h] = totals[h] + dq_in[i, h * half:(h + 1) * half].astype(F32)
    for h in range(2):
        gq_ref[h * half:(h + 1) * half] = (totals[h] * scale).astype(BF16)

    for cp in sends:
        cp.wait_send()

    @pl.when(jnp.logical_not(to_self))
    def _():
        m_copy.wait_send()

    @pl.when(collects)
    def _():
        for cp in mb_copies:
            cp.wait_send()


def shards(queries, key_vectors, value_vectors, outputs, out_grad, logsumexp, positions):
    shard, width = queries.shape
    half = shard // 2
    vmem = pl.BlockSpec(memory_space=pltpu.VMEM)
    dma = pltpu.SemaphoreType.DMA
    return pl.pallas_call(
        functools.partial(kernel, half),
        name="attention_backward",
        out_shape=[jax.ShapeDtypeStruct((shard, width), BF16)] * 3,
        in_specs=[pl.BlockSpec(memory_space=pltpu.HBM)] * 7,
        out_specs=[vmem] * 3,
        scratch_shapes=[
            pltpu.VMEM((4, 8, 2 * shard + 16, width), BF16),
            pltpu.VMEM((16, 2 * shard, width), BF16),
            pltpu.VMEM((shard, width), BF16),
            pltpu.VMEM((1, shard), F32),
            pltpu.VMEM((1, shard), jnp.int32),
            pltpu.VMEM((8, 128), F32),
            pltpu.VMEM((1, 128), F32),
            pltpu.VMEM((16, 1, 128), F32),
            pltpu.VMEM((2, 16 * half, 128), F32),
            pltpu.VMEM((4, 8, 8 * half), F32),
            pltpu.VMEM((4, 2, 8, half, width), F32),
            pltpu.VMEM((2, 16 * half, width), F32),
            pltpu.VMEM((2, 16 * half, width), F32),
            pltpu.VMEM((4, 4, shard, width), BF16),
            pltpu.VMEM((4, 4, shard, width), BF16),
            pltpu.VMEM((4, 4, shard, width), BF16),
            pltpu.VMEM((4, 4, shard, width), BF16),
            pltpu.VMEM((len(FINAL), shard, width), BF16),
            pltpu.VMEM((15, 2, 2, half, width), BF16),
            pltpu.VMEM((15, 2, 2, half, width), BF16),
            dma((7,)),
            dma((160,)),
            dma((2, 16)),
            dma((16,)),
            dma((15,)),
            dma((16,)),
            dma((1,)),
            dma((4,)),
            dma((4, 4)),
            dma((len(FINAL),)),
            dma((15, 2)),
        ],
        compiler_params=pltpu.CompilerParams(
            collective_id=0, has_side_effects=True, vmem_limit_bytes=48 * 2 ** 20
        ),
    )(
        queries, key_vectors, value_vectors, outputs, out_grad,
        logsumexp.reshape(1, shard), positions.reshape(1, shard),
    )


def solution(mesh):
    in_specs = (
        P(("row", "col"), None),
        P(("col", "row"), None),
        P(("col", "row"), None),
        P(("row", "col"), None),
        P(("row", "col"), None),
        P(("row", "col")),
        P(("row", "col")),
    )
    out_specs = (P(("row", "col"), None), P(("col", "row"), None), P(("col", "row"), None))
    return jax.shard_map(shards, mesh=mesh, in_specs=in_specs, out_specs=out_specs, check_vma=False)
```

```python
import functools

import jax
import jax.numpy as jnp
from jax import lax
from jax.experimental import pallas as pl
from jax.experimental.pallas import tpu as pltpu
from jax.sharding import PartitionSpec as P

MESH = pl.DeviceIdType.MESH
F32 = jnp.float32
BF16 = jnp.bfloat16
NT = (((1,), (1,)), ((), ()))
NN = (((1,), (0,)), ((), ()))
TN = (((0,), (0,)), ((), ()))
LOG2E = 1.4426950408889634

ROUNDS = ((0, -1, 1, 2), (-2, 3, -3, 4), (-4, 5, -5, 6), (-6, 7, -7, 8))
ROUND_OF = {o: r for r, offs in enumerate(ROUNDS) for o in offs}
HAND_ON = {8: 6, 7: 5, -7: -5, -6: -4, 4: 3, -3: -2, 2: 1}
TAKES = {b: a for a, b in HAND_ON.items()}
FINAL = tuple(o for offs in ROUNDS for o in offs if o != 0 and o not in HAND_ON)
PLANE = [(a, b) for b in (0, 1, 3, 2) for a in (1, 3, 2, 0) if (a, b) != (0, 0)]


def dot(a, b, dims):
    return lax.dot_general(a, b, dims, preferred_element_type=F32)


def device(x, y, z, core):
    return (lax.rem(z, 8) * 4 + x, (y * 2 + z // 8) * 2 + core)


def kernel(
    half, q_hbm, k_hbm, v_hbm, o_hbm, do_hbm, lse_hbm, pos_hbm,
    gq_ref, gk_ref, gv_ref,
    qbuf, kbuf, o_ref, lse_ref, pos_ref, rowbuf, mrow, mstage, mbuf, pk, rows, dq, dk, dv,
    sib_out, sib_in, dq_out, pair_in, dq_in, kv_out, kv_in,
    in_sem, send_sem, q_recv, qs_recv, k_recv, ms_recv, m_recv, mb_recv, sib_recv, pair_recv, dq_recv, kv_recv,
):
    width = q_hbm.shape[1]
    shard = 2 * half
    scale = width ** -0.5
    row, col = lax.axis_index("row"), lax.axis_index("col")
    z_lo, x = row // 4, lax.rem(row, 4)
    core, z_hi, y = lax.rem(col, 2), lax.rem(col // 2, 2), col // 4
    z = z_hi * 8 + z_lo
    other = 1 - core

    def at_z(o):
        return device(x, y, lax.rem(z + o + 16, 16), core)

    def at_plane(a, b):
        return device(lax.rem(x + a, 4), lax.rem(y + b, 4), z, core)

    sibling = device(x, y, z, other)

    to_z = lax.rem(z, 2) * 8 + lax.rem(x, 2) * 4 + y
    to_core = x // 2
    to_self = jnp.logical_and(to_z == z, to_core == core)
    my_mslot = (z_hi * 2 + core) * 4 + z_lo // 2
    collects = jnp.logical_and(x == core * 2 + z_lo // 4, y == lax.rem(z_lo, 4))

    def holder(slot):
        xo, yo = slot // 4, slot % 4
        hz, hc = (xo // 2) * 8 + 2 * yo + z_hi, xo % 2
        return hz, hc, jnp.logical_and(hz == z, hc == core)

    my_qslot = lax.rem(z, 4) * 2 + core
    my_kslot = x * 4 + y
    inputs = [
        pltpu.make_async_copy(src, dst, in_sem.at[i])
        for i, (src, dst) in enumerate((
            (do_hbm, qbuf.at[0, my_qslot, pl.ds(shard, shard)]),
            (o_hbm, o_ref),
            (lse_hbm, lse_ref),
            (pos_hbm, pos_ref),
            (q_hbm, qbuf.at[0, my_qslot, pl.ds(0, shard)]),
            (k_hbm, kbuf.at[my_kslot, pl.ds(0, shard)]),
            (v_hbm, kbuf.at[my_kslot, pl.ds(shard, shard)]),
        ))
    ]
    for cp in inputs:
        cp.start()

    barrier = pltpu.get_barrier_semaphore()
    greeted = [at_plane(a, b) for a, b in PLANE] + [sibling]
    for o in (-4, -3, -2, -1, 1, 2, 3, 4):
        greeted += [at_z(o), device(x, y, lax.rem(z + o + 16, 16), other)]
    for target in greeted:
        pl.semaphore_signal(barrier, inc=1, device_id=target, device_id_type=MESH)

    sends = []

    def send(src, dst, recv_sem, target):
        cp = pltpu.make_async_remote_copy(
            src_ref=src, dst_ref=dst, send_sem=send_sem.at[len(sends)], recv_sem=recv_sem,
            device_id=target, device_id_type=MESH,
        )
        sends.append(cp)
        cp.start()

    def arrived(dst, recv_sem):
        pltpu.make_async_remote_copy(
            src_ref=dst, dst_ref=dst, send_sem=send_sem.at[0], recv_sem=recv_sem,
            device_id=sibling, device_id_type=MESH,
        ).wait_recv()

    for cp in inputs:
        cp.wait()
    prod = qbuf[0, my_qslot, shard:2 * shard].astype(F32) * o_ref[...].astype(F32)
    rowbuf[...] = jnp.zeros_like(rowbuf)
    rowbuf[0:1, 0:shard] = lse_ref[...] * LOG2E
    rowbuf[1:2, 0:shard] = jnp.sum(prod.T, axis=0, keepdims=True)
    base = jnp.broadcast_to(pos_ref[0:1, 0:1].astype(F32), (1, 128))
    mrow[...] = base
    shift = lax.rem(my_qslot * half, 128)
    early = pltpu.roll(rowbuf[...], shift, 1)
    late = pltpu.roll(rowbuf[...], lax.rem(shift + 128 - half, 128), 1)
    sub = lax.broadcasted_iota(jnp.int32, (8, 128), 0)
    full = jnp.where(
        sub < 2, early,
        jnp.where(sub < 4, pltpu.roll(late, 2, 0), jnp.where(sub == 4, jnp.broadcast_to(base, (8, 128)), 0.0)),
    )
    hi = full.astype(BF16).astype(F32)
    mid = (full - hi).astype(BF16).astype(F32)
    qbuf[0, my_qslot, 2 * shard:2 * shard + 16] = jnp.concatenate([hi, mid], axis=0).astype(BF16)

    pl.semaphore_wait(barrier, len(greeted))

    def qslot(o):
        return lax.rem(z + o + 16, 4) * 2 + core

    def sslot(o):
        return lax.rem(z + o + 16, 4) * 2 + other

    chunks = (pl.ds(0, shard), pl.ds(shard, shard + 16))

    def directions(o):
        return (1, -1) if o == 0 else ((1,) if o < 0 else (-1,))

    def relay(o, c):
        for sign in directions(o):
            there = o - sign * 2
            if there in ROUND_OF:
                send(
                    qbuf.at[ROUND_OF[o], qslot(o), chunks[c]],
                    qbuf.at[ROUND_OF[there], qslot(o), chunks[c]],
                    q_recv.at[c, there + 7], at_z(sign * 2),
                )

    def deliver(o):
        for sign in directions(o):
            there = o - sign
            send(
                qbuf.at[ROUND_OF[o], qslot(o)], qbuf.at[ROUND_OF[there], qslot(o)],
                q_recv.at[1, there + 7], at_z(sign),
            )

    def to_sibling(o):
        ref = qbuf.at[ROUND_OF[o], qslot(o)]
        send(ref, ref, qs_recv.at[o + 7], sibling)

    def take(o, c):
        arrived(qbuf.at[ROUND_OF[o], qslot(o), chunks[c]], q_recv.at[c, o + 7])

    def take_whole(o):
        arrived(qbuf.at[ROUND_OF[o], qslot(o)], q_recv.at[1, o + 7])

    def keys_out(first, last):
        for i in range(first, last):
            ref = kbuf.at[my_kslot]
            send(ref, ref, k_recv.at[i], at_plane(*PLANE[i]))

    relay(0, 0)
    relay(0, 1)
    to_sibling(0)
    deliver(0)
    keys_out(0, 15)

    ahead = lax.rem(to_z - z + 16, 16)
    ahead = jnp.where(ahead > 8, ahead - 16, ahead)
    last = send_sem.shape[0] - 1

    m_direct = pltpu.make_async_remote_copy(
        src_ref=mrow, dst_ref=mbuf.at[my_mslot], send_sem=send_sem.at[last],
        recv_sem=m_recv.at[my_mslot], device_id=device(x, y, to_z, to_core), device_id_type=MESH,
    )
    m_first = {
        sign: pltpu.make_async_remote_copy(
            src_ref=mrow, dst_ref=mstage.at[2 * j + core], send_sem=send_sem.at[last],
            recv_sem=ms_recv.at[2 * j + core],
            device_id=device(x, y, lax.rem(z + 4 * sign + 16, 16), to_core), device_id_type=MESH,
        )
        for j, sign in enumerate((1, -1))
    }
    m_onward = []
    for j, sign in enumerate((1, -1)):
        for hc in range(2):
            hz = lax.rem(z - 4 * sign + 16, 16)
            far = lax.rem(to_z - hz + 16, 16)
            far = jnp.where(far > 8, far - 16, far)
            mslot = (hz // 8 * 2 + hc) * 4 + lax.rem(hz, 8) // 2
            m_onward.append((
                jnp.logical_and(core == to_core, far * sign > 4),
                pltpu.make_async_remote_copy(
                    src_ref=mstage.at[2 * j + hc], dst_ref=mbuf.at[mslot], send_sem=send_sem.at[last - 16 - 2 * j - hc],
                    recv_sem=m_recv.at[mslot], device_id=device(x, y, to_z, to_core), device_id_type=MESH,
                ),
            ))
    m_near = jnp.logical_and(jnp.logical_not(to_self), jnp.abs(ahead) <= 4)

    @pl.when(m_near)
    def _():
        m_direct.start()

    for sign in (1, -1):

        @pl.when(ahead * sign > 4)
        def _():
            m_first[sign].start()

    @pl.when(to_self)
    def _():
        mbuf[my_mslot] = mrow[...]

    lane = lax.broadcasted_iota(jnp.int32, (8, 128), 1)

    def unpack(r):
        tiles = []
        pieces = []
        for s in range(8):
            raw = qbuf[r, s, 2 * shard:2 * shard + 16].astype(F32)
            pieces.append(raw[0:8] + raw[8:16])
        for j in range(8 * half // 128):
            first, last = 128 * j // half, (128 * j + 127) // half
            tile = pieces[last]
            for s in range(last - 1, first - 1, -1):
                tile = jnp.where(lane < (s + 1) * half - 128 * j, pieces[s], tile)
            tiles.append(tile)
        rows[r] = jnp.concatenate(tiles, axis=1)

    nq = 8 * half
    nk = 8 * half
    lanes = lax.broadcasted_iota(jnp.int32, (1, nq), 1).astype(F32)
    offs = lanes - half * jnp.floor((lanes + 0.5) * (1.0 / half))
    top = 1023.0 * half

    def block(r, kh, qh, kb, masked, first_q, first_k):
        k = kbuf[8 * kb:8 * kb + 8, kh * half:(kh + 1) * half].reshape(nk, width)
        v = kbuf[8 * kb:8 * kb + 8, shard + kh * half:shard + (kh + 1) * half].reshape(nk, width)
        q = qbuf[r, :, qh * half:(qh + 1) * half].reshape(nq, width)
        do = qbuf[r, :, shard + qh * half:shard + (qh + 1) * half].reshape(nq, width)
        lse = rows[r, 2 * qh:2 * qh + 1]
        delta = rows[r, 2 * qh + 1:2 * qh + 2]
        s = dot(k, q, NT)
        dp = dot(v, do, NT)
        p = jnp.exp2(s * (scale * LOG2E) - lse)
        if masked:
            start = rows[r, 4:5]
            pq = (start if qh == 0 else top - start) + offs
            pkk = jnp.concatenate([pk[kh, nk * kb:nk * (kb + 1)]] * (nq // 128), axis=1)
            p = jnp.where(pkk <= pq, p, 0.0)
        ds = (p * (dp - delta)).astype(BF16)
        ph = p.astype(BF16)
        gv, gk, gq = dot(ph, do, NN), dot(ds, q, NN), dot(ds, k, TN)
        span = slice(nk * kb, nk * (kb + 1))
        if first_k:
            dv[kh, span] = gv
            dk[kh, span] = gk
        else:
            dv[kh, span] += gv
            dk[kh, span] += gk
        gq = gq.reshape(8, half, width)
        if first_q:
            dq[r, qh] = gq
        else:
            dq[r, qh] += gq

    def late_early(r, first):
        for kb in range(2):
            block(r, 0, 1, kb, False, kb == 0, first)

    def early_early(r):
        for kb in range(2):
            block(r, 0, 0, kb, True, kb == 0, False)

    def late_late(r, first):
        for kb in range(2):
            block(r, 1, 1, kb, True, False, first)

    def ready(r):
        for o in ROUNDS[r]:
            arrived(qbuf.at[r, sslot(o)], qs_recv.at[o + 7])
        unpack(r)

    def stage(k):
        far = [o for o in (-2 * k, 2 * k) if o in ROUND_OF]
        for c in range(2):
            for o in far:
                take(o, c)
                if k < 4:
                    relay(o, c)
        for o in far:
            if k < 4:
                deliver(o)
            to_sibling(o)
        for o in (-2 * k + 1, 2 * k - 1):
            take_whole(o)
            to_sibling(o)

    def share(r):
        for i, o in enumerate(ROUNDS[r]):
            sib_out[r, i, 0:half] = dq[r, 0, sslot(o)].astype(BF16)
            sib_out[r, i, half:shard] = dq[r, 1, sslot(o)].astype(BF16)
        send(sib_out.at[r], sib_in.at[r], sib_recv.at[r], sibling)

    def home_far(r):
        arrived(sib_in.at[r], sib_recv.at[r])
        for i, o in enumerate(ROUNDS[r]):
            if o in HAND_ON or (o != 0 and o not in TAKES):
                for h in range(2):
                    span = slice(h * half, (h + 1) * half)
                    dq_out[r, i, span] = (dq[r, h, qslot(o)] + sib_in[r, i, span].astype(F32)).astype(BF16)
                if o not in HAND_ON:
                    send(dq_out.at[r, i], dq_in.at[FINAL.index(o)], dq_recv.at[FINAL.index(o)], at_z(o))
                else:
                    there = HAND_ON[o]
                    rt = ROUND_OF[there]
                    j = ROUNDS[rt].index(there)
                    send(dq_out.at[r, i], pair_in.at[rt, j], pair_recv.at[rt, j], at_z(o - there))

    def home_near(r):
        for i, o in enumerate(ROUNDS[r]):
            if o in TAKES or o == 0:
                if o != 0:
                    arrived(pair_in.at[r, i], pair_recv.at[r, i])
                for h in range(2):
                    span = slice(h * half, (h + 1) * half)
                    total = dq[r, h, qslot(o)] + sib_in[r, i, span].astype(F32)
                    if o == 0:
                        dq[r, h, qslot(o)] = total
                    else:
                        dq_out[r, i, span] = (total + pair_in[r, i, span].astype(F32)).astype(BF16)
                if o != 0:
                    send(dq_out.at[r, i], dq_in.at[FINAL.index(o)], dq_recv.at[FINAL.index(o)], at_z(o))

    def keys_home(h):
        for i, (a, b) in enumerate(PLANE):
            slot = lax.rem(x + a, 4) * 4 + lax.rem(y + b, 4)
            span = pl.ds(pl.multiple_of(slot * half, 16), half)
            kv_out[i, h, 0] = dk[h, span].astype(BF16)
            kv_out[i, h, 1] = dv[h, span].astype(BF16)
            send(kv_out.at[i, h], kv_in.at[i, h], kv_recv.at[i, h], at_plane(a, b))

    stage(1)

    for i, (used, cp) in enumerate(m_onward):

        @pl.when(used)
        def _():
            arrived(mstage.at[i], ms_recv.at[i])
            cp.start()

    ready(0)
    stage(2)
    ready(1)

    for slot in range(16):
        hz, hc, mine = holder(slot)

        @pl.when(jnp.logical_and(collects, jnp.logical_not(mine)))
        def _():
            arrived(mbuf.at[slot], m_recv.at[slot])

    mb_copies = [
        pltpu.make_async_remote_copy(
            src_ref=mbuf, dst_ref=mbuf, send_sem=send_sem.at[send_sem.shape[0] - 2 - i],
            recv_sem=mb_recv.at[0], device_id=at_plane(a, b), device_id_type=MESH,
        )
        for i, (a, b) in enumerate(PLANE)
    ]

    @pl.when(collects)
    def _():
        for cp in mb_copies:
            cp.start()

    for i, (a, b) in enumerate(PLANE):
        arrived(kbuf.at[lax.rem(x - a + 4, 4) * 4 + lax.rem(y - b + 4, 4)], k_recv.at[i])
    late_early(0, True)
    late_early(1, False)
    stage(3)
    ready(2)
    late_early(2, False)

    @pl.when(jnp.logical_not(collects))
    def _():
        arrived(mbuf, mb_recv.at[0])

    sub48 = lax.broadcasted_iota(jnp.int32, (half, 128), 0).astype(F32)
    for slot in range(16):
        start = jnp.broadcast_to(mbuf[slot], (half, 128))
        pk[0, slot * half:(slot + 1) * half] = start + sub48
        pk[1, slot * half:(slot + 1) * half] = top - start + sub48

    early_early(0)
    late_late(0, True)
    share(0)
    early_early(1)
    late_late(1, False)
    share(1)
    home_far(0)
    stage(4)
    home_near(0)
    home_far(1)
    ready(3)
    late_early(3, False)
    early_early(3)
    late_late(3, False)
    share(3)
    home_near(1)
    early_early(2)
    keys_home(0)
    home_far(3)
    late_late(2, False)
    share(2)
    keys_home(1)
    arrived(sib_in.at[2], sib_recv.at[2])
    home_near(2)

    for h in range(2):
        span = pl.ds(pl.multiple_of(my_kslot * half, 16), half)
        rowspan = slice(h * half, (h + 1) * half)
        sk, sv = dk[h, span], dv[h, span]
        for i in range(15):
            arrived(kv_in.at[i, h], kv_recv.at[i, h])
            sk = sk + kv_in[i, h, 0].astype(F32)
            sv = sv + kv_in[i, h, 1].astype(F32)
        gk_ref[rowspan] = (sk * scale).astype(BF16)
        gv_ref[rowspan] = sv.astype(BF16)

    totals = [dq[0, h, my_qslot] for h in range(2)]
    for i in range(len(FINAL)):
        arrived(dq_in.at[i], dq_recv.at[i])
        for h in range(2):
            totals[h] = totals[h] + dq_in[i, h * half:(h + 1) * half].astype(F32)
    for h in range(2):
        gq_ref[h * half:(h + 1) * half] = (totals[h] * scale).astype(BF16)

    for cp in sends:
        cp.wait_send()

    @pl.when(m_near)
    def _():
        m_direct.wait_send()

    for sign in (1, -1):

        @pl.when(ahead * sign > 4)
        def _():
            m_first[sign].wait_send()

    for used, cp in m_onward:

        @pl.when(used)
        def _():
            cp.wait_send()

    @pl.when(collects)
    def _():
        for cp in mb_copies:
            cp.wait_send()


def shards(queries, key_vectors, value_vectors, outputs, out_grad, logsumexp, positions):
    shard, width = queries.shape
    half = shard // 2
    vmem = pl.BlockSpec(memory_space=pltpu.VMEM)
    dma = pltpu.SemaphoreType.DMA
    return pl.pallas_call(
        functools.partial(kernel, half),
        name="attention_backward",
        out_shape=[jax.ShapeDtypeStruct((shard, width), BF16)] * 3,
        in_specs=[pl.BlockSpec(memory_space=pltpu.HBM)] * 7,
        out_specs=[vmem] * 3,
        scratch_shapes=[
            pltpu.VMEM((4, 8, 2 * shard + 16, width), BF16),
            pltpu.VMEM((16, 2 * shard, width), BF16),
            pltpu.VMEM((shard, width), BF16),
            pltpu.VMEM((1, shard), F32),
            pltpu.VMEM((1, shard), jnp.int32),
            pltpu.VMEM((8, 128), F32),
            pltpu.VMEM((1, 128), F32),
            pltpu.VMEM((4, 1, 128), F32),
            pltpu.VMEM((16, 1, 128), F32),
            pltpu.VMEM((2, 16 * half, 128), F32),
            pltpu.VMEM((4, 8, 8 * half), F32),
            pltpu.VMEM((4, 2, 8, half, width), F32),
            pltpu.VMEM((2, 16 * half, width), F32),
            pltpu.VMEM((2, 16 * half, width), F32),
            pltpu.VMEM((4, 4, shard, width), BF16),
            pltpu.VMEM((4, 4, shard, width), BF16),
            pltpu.VMEM((4, 4, shard, width), BF16),
            pltpu.VMEM((4, 4, shard, width), BF16),
            pltpu.VMEM((len(FINAL), shard, width), BF16),
            pltpu.VMEM((15, 2, 2, half, width), BF16),
            pltpu.VMEM((15, 2, 2, half, width), BF16),
            dma((7,)),
            dma((160,)),
            dma((2, 16)),
            dma((16,)),
            dma((15,)),
            dma((4,)),
            dma((16,)),
            dma((1,)),
            dma((4,)),
            dma((4, 4)),
            dma((len(FINAL),)),
            dma((15, 2)),
        ],
        compiler_params=pltpu.CompilerParams(
            collective_id=0, has_side_effects=True, vmem_limit_bytes=60 * 2 ** 20
        ),
    )(
        queries, key_vectors, value_vectors, outputs, out_grad,
        logsumexp.reshape(1, shard), positions.reshape(1, shard),
    )


def solution(mesh):
    in_specs = (
        P(("row", "col"), None),
        P(("col", "row"), None),
        P(("col", "row"), None),
        P(("row", "col"), None),
        P(("row", "col"), None),
        P(("row", "col")),
        P(("row", "col")),
    )
    out_specs = (P(("row", "col"), None), P(("col", "row"), None), P(("col", "row"), None))
    return jax.shard_map(shards, mesh=mesh, in_specs=in_specs, out_specs=out_specs, check_vma=False)
```

```python
import functools

import jax
import jax.numpy as jnp
from jax import lax
from jax.experimental import pallas as pl
from jax.experimental.pallas import tpu as pltpu
from jax.sharding import PartitionSpec as P

MESH = pl.DeviceIdType.MESH
F32 = jnp.float32
BF16 = jnp.bfloat16
NT = (((1,), (1,)), ((), ()))
NN = (((1,), (0,)), ((), ()))
TN = (((0,), (0,)), ((), ()))
LOG2E = 1.4426950408889634

ROUNDS = ((0, -1, 1, 2), (-2, 3, -3, 4), (-4, 5, -5, 6), (-6, 7, -7, 8))
ROUND_OF = {o: r for r, offs in enumerate(ROUNDS) for o in offs}
HAND_ON = {8: 6, 7: 5, -7: -5, -6: -4, 4: 3, -3: -2, 2: 1}
TAKES = {b: a for a, b in HAND_ON.items()}
FINAL = tuple(o for offs in ROUNDS for o in offs if o != 0 and o not in HAND_ON)
PLANE = (
    (2, 2), (3, 2), (2, 1), (0, 2), (1, 2), (3, 1), (2, 3), (0, 1), (1, 1), (3, 3), (1, 3), (0, 3), (2, 0), (3, 0), (1, 0),
)
PAIRS = tuple(sorted(set(HAND_ON.values())))
CHUNK, DELIVER, SIBLING, KEYS, SHARE, HOME, KEYS_HOME, M_FIRST, M_LAST, M_ONWARD = 0, 2, 3, 4, 5, 6, 7, 8, 9, 10


def q_index(o, c):
    return (o + 7) // 2 if o % 2 else 8 + (o // 2 + (3 if o < 0 else 2)) * 2 + c


def dot(a, b, dims):
    return lax.dot_general(a, b, dims, preferred_element_type=F32)


def device(x, y, z, core):
    return (lax.rem(z, 8) * 4 + x, (y * 2 + z // 8) * 2 + core)


def kernel(
    half, q_hbm, k_hbm, v_hbm, o_hbm, do_hbm, lse_hbm, pos_hbm,
    out_ref,
    qbuf, kbuf, o_ref, lse_ref, pos_ref, rowbuf, mrow, mstage, mbuf, mwide, pk, rows, dq, dk, dv,
    sib_out, sib_in, dq_out, pair_in, dq_in, kv_out, kv_in,
    in_sem, send_sem, q_recv, qs_recv, k_recv, ms_recv, m_recv, mb_recv, sib_recv, pair_recv, dq_recv, kv_recv,
):
    width = q_hbm.shape[1]
    shard = 2 * half
    scale = width ** -0.5
    row, col = lax.axis_index("row"), lax.axis_index("col")
    z_lo, x = row // 4, lax.rem(row, 4)
    core, z_hi, y = lax.rem(col, 2), lax.rem(col // 2, 2), col // 4
    z = z_hi * 8 + z_lo
    other = 1 - core

    def at_z(o):
        return device(x, y, lax.rem(z + o + 16, 16), core)

    def at_plane(a, b):
        return device(lax.rem(x + a, 4), lax.rem(y + b, 4), z, core)

    sibling = device(x, y, z, other)

    to_z = lax.rem(z, 2) * 8 + lax.rem(x, 2) * 4 + y
    to_core = x // 2
    to_self = jnp.logical_and(to_z == z, to_core == core)
    my_mslot = (z_hi * 2 + core) * 4 + z_lo // 2
    collects = jnp.logical_and(x == core * 2 + z_lo // 4, y == lax.rem(z_lo, 4))

    my_qslot = lax.rem(z, 4) * 2 + core
    my_kslot = x * 4 + y
    inputs = [
        pltpu.make_async_copy(src, dst, in_sem.at[i])
        for i, (src, dst) in enumerate((
            (do_hbm, qbuf.at[0, my_qslot, pl.ds(shard, shard)]),
            (o_hbm, o_ref),
            (lse_hbm, lse_ref),
            (pos_hbm, pos_ref),
            (q_hbm, qbuf.at[0, my_qslot, pl.ds(0, shard)]),
            (k_hbm, kbuf.at[my_kslot, pl.ds(0, shard)]),
            (v_hbm, kbuf.at[my_kslot, pl.ds(shard, shard)]),
        ))
    ]
    for cp in inputs:
        cp.start()

    barrier = pltpu.get_barrier_semaphore()
    greeted = [at_plane(a, b) for a, b in PLANE] + [sibling]
    for o in (-4, -3, -2, -1, 1, 2, 3, 4):
        greeted += [at_z(o), device(x, y, lax.rem(z + o + 16, 16), other)]
    for target in greeted:
        pl.semaphore_signal(barrier, inc=1, device_id=target, device_id_type=MESH)

    def send(kind, src, dst, recv_sem, target):
        pltpu.make_async_remote_copy(
            src_ref=src, dst_ref=dst, send_sem=send_sem.at[kind], recv_sem=recv_sem,
            device_id=target, device_id_type=MESH,
        ).start()

    def sent(kind, whole):
        pltpu.make_async_remote_copy(
            src_ref=whole, dst_ref=whole, send_sem=send_sem.at[kind], recv_sem=mb_recv.at[0],
            device_id=sibling, device_id_type=MESH,
        ).wait_send()

    def arrived(dst, recv_sem):
        pltpu.make_async_remote_copy(
            src_ref=dst, dst_ref=dst, send_sem=send_sem.at[0], recv_sem=recv_sem,
            device_id=sibling, device_id_type=MESH,
        ).wait_recv()

    for cp in inputs:
        cp.wait()
    prod = qbuf[0, my_qslot, shard:2 * shard].astype(F32) * o_ref[...].astype(F32)
    rowbuf[...] = jnp.zeros_like(rowbuf)
    rowbuf[0:1, 0:shard] = lse_ref[...] * LOG2E
    rowbuf[1:2, 0:shard] = jnp.sum(prod.T, axis=0, keepdims=True)
    base = jnp.broadcast_to(pos_ref[0:1, 0:1].astype(F32), (1, 128))
    mrow[...] = base
    shift = lax.rem(my_qslot * half, 128)
    early = pltpu.roll(rowbuf[...], shift, 1)
    late = pltpu.roll(rowbuf[...], lax.rem(shift + 128 - half, 128), 1)
    sub = lax.broadcasted_iota(jnp.int32, (8, 128), 0)
    full = jnp.where(
        sub < 2, early,
        jnp.where(sub < 4, pltpu.roll(late, 2, 0), jnp.where(sub == 4, jnp.broadcast_to(base, (8, 128)), 0.0)),
    )
    hi = full.astype(BF16).astype(F32)
    mid = (full - hi).astype(BF16).astype(F32)
    qbuf[0, my_qslot, 2 * shard:2 * shard + 16] = jnp.concatenate([hi, mid], axis=0).astype(BF16)

    pl.semaphore_wait(barrier, len(greeted))

    def qslot(o):
        return lax.rem(z + o + 16, 4) * 2 + core

    def sslot(o):
        return lax.rem(z + o + 16, 4) * 2 + other

    chunks = (pl.ds(0, shard), pl.ds(shard, shard + 16))

    def directions(o):
        return (1, -1) if o == 0 else ((1,) if o < 0 else (-1,))

    def relay(o, c):
        for sign in directions(o):
            there = o - sign * 2
            if there in ROUND_OF:
                send(
                    CHUNK + c, qbuf.at[ROUND_OF[o], qslot(o), chunks[c]],
                    qbuf.at[ROUND_OF[there], qslot(o), chunks[c]],
                    q_recv.at[q_index(there, c)], at_z(sign * 2),
                )

    def deliver(o):
        for sign in directions(o):
            there = o - sign
            send(
                DELIVER, qbuf.at[ROUND_OF[o], qslot(o)], qbuf.at[ROUND_OF[there], qslot(o)],
                q_recv.at[q_index(there, 1)], at_z(sign),
            )

    def to_sibling(o):
        ref = qbuf.at[ROUND_OF[o], qslot(o)]
        send(SIBLING, ref, ref, qs_recv.at[ROUND_OF[o]], sibling)

    def take(o, c):
        arrived(qbuf.at[ROUND_OF[o], qslot(o), chunks[c]], q_recv.at[q_index(o, c)])

    def take_whole(o):
        arrived(qbuf.at[ROUND_OF[o], qslot(o)], q_recv.at[q_index(o, 1)])

    def keys_out(first, last):
        for i in range(first, last):
            ref = kbuf.at[my_kslot]
            send(KEYS, ref, ref, k_recv.at[0], at_plane(*PLANE[i]))

    relay(0, 0)
    relay(0, 1)
    to_sibling(0)
    deliver(0)
    keys_out(0, 15)

    ahead = lax.rem(to_z - z + 16, 16)
    ahead = jnp.where(ahead > 8, ahead - 16, ahead)

    m_direct = pltpu.make_async_remote_copy(
        src_ref=mrow, dst_ref=mbuf.at[my_mslot], send_sem=send_sem.at[M_FIRST],
        recv_sem=m_recv.at[0], device_id=device(x, y, to_z, to_core), device_id_type=MESH,
    )
    m_first = {
        sign: pltpu.make_async_remote_copy(
            src_ref=mrow, dst_ref=mstage.at[2 * j + core], send_sem=send_sem.at[M_FIRST],
            recv_sem=ms_recv.at[2 * j + core],
            device_id=device(x, y, lax.rem(z + 4 * sign + 16, 16), to_core), device_id_type=MESH,
        )
        for j, sign in enumerate((1, -1))
    }
    m_onward = []
    for j, sign in enumerate((1, -1)):
        for hc in range(2):
            hz = lax.rem(z - 4 * sign + 16, 16)
            far = lax.rem(to_z - hz + 16, 16)
            far = jnp.where(far > 8, far - 16, far)
            mslot = (hz // 8 * 2 + hc) * 4 + lax.rem(hz, 8) // 2
            m_onward.append((
                jnp.logical_and(core == to_core, far * sign > 4),
                pltpu.make_async_remote_copy(
                    src_ref=mstage.at[2 * j + hc], dst_ref=mbuf.at[mslot], send_sem=send_sem.at[M_ONWARD + 2 * j + hc],
                    recv_sem=m_recv.at[0], device_id=device(x, y, to_z, to_core), device_id_type=MESH,
                ),
            ))
    m_near = jnp.logical_and(jnp.logical_not(to_self), jnp.abs(ahead) <= 4)

    @pl.when(m_near)
    def _():
        m_direct.start()

    for sign in (1, -1):

        @pl.when(ahead * sign > 4)
        def _():
            m_first[sign].start()

    @pl.when(to_self)
    def _():
        mbuf[my_mslot] = mrow[...]

    lane = lax.broadcasted_iota(jnp.int32, (8, 128), 1)

    def unpack(r):
        tiles = []
        pieces = []
        for s in range(8):
            raw = qbuf[r, s, 2 * shard:2 * shard + 16].astype(F32)
            pieces.append(raw[0:8] + raw[8:16])
        for j in range(8 * half // 128):
            first, last = 128 * j // half, (128 * j + 127) // half
            tile = pieces[last]
            for s in range(last - 1, first - 1, -1):
                tile = jnp.where(lane < (s + 1) * half - 128 * j, pieces[s], tile)
            tiles.append(tile)
        rows[r] = jnp.concatenate(tiles, axis=1)

    nq = 8 * half
    nk = 8 * half
    lanes = lax.broadcasted_iota(jnp.int32, (1, nq), 1).astype(F32)
    offs = lanes - half * jnp.floor((lanes + 0.5) * (1.0 / half))
    top = 1023.0 * half

    def block(r, kh, qh, kb, masked, first_q, first_k):
        k = kbuf[8 * kb:8 * kb + 8, kh * half:(kh + 1) * half].reshape(nk, width)
        v = kbuf[8 * kb:8 * kb + 8, shard + kh * half:shard + (kh + 1) * half].reshape(nk, width)
        q = qbuf[r, :, qh * half:(qh + 1) * half].reshape(nq, width)
        do = qbuf[r, :, shard + qh * half:shard + (qh + 1) * half].reshape(nq, width)
        lse = rows[r, 2 * qh:2 * qh + 1]
        delta = rows[r, 2 * qh + 1:2 * qh + 2]
        s = dot(k, q, NT)
        dp = dot(v, do, NT)
        p = jnp.exp2(s * (scale * LOG2E) - lse)
        if masked:
            start = rows[r, 4:5]
            pq = (start if qh == 0 else top - start) + offs
            pkk = jnp.concatenate([pk[kh, nk * kb:nk * (kb + 1)]] * (nq // 128), axis=1)
            p = jnp.where(pkk <= pq, p, 0.0)
        ds = (p * (dp - delta)).astype(BF16)
        ph = p.astype(BF16)
        gv, gk, gq = dot(ph, do, NN), dot(ds, q, NN), dot(ds, k, TN)
        span = slice(nk * kb, nk * (kb + 1))
        if first_k:
            dv[kh, span] = gv
            dk[kh, span] = gk
        else:
            dv[kh, span] += gv
            dk[kh, span] += gk
        gq = gq.reshape(8, half, width)
        if first_q:
            dq[r, qh] = gq
        else:
            dq[r, qh] += gq

    def late_early(r, first):
        for kb in range(2):
            block(r, 0, 1, kb, False, kb == 0, first)

    def early_early(r):
        for kb in range(2):
            block(r, 0, 0, kb, True, kb == 0, False)

    def late_late(r, first):
        for kb in range(2):
            block(r, 1, 1, kb, True, False, first)

    def ready(r):
        arrived(qbuf.at[r, pl.ds(0, 4)], qs_recv.at[r])
        unpack(r)

    def stage(k):
        far = [o for o in (-2 * k, 2 * k) if o in ROUND_OF]
        for c in range(2):
            for o in far:
                take(o, c)
                if k < 4:
                    relay(o, c)
        for o in far:
            if k < 4:
                deliver(o)
            to_sibling(o)
        for o in (-2 * k + 1, 2 * k - 1):
            take_whole(o)
            to_sibling(o)

    def share(r):
        for i, o in enumerate(ROUNDS[r]):
            sib_out[r, i, 0:half] = dq[r, 0, sslot(o)].astype(BF16)
            sib_out[r, i, half:shard] = dq[r, 1, sslot(o)].astype(BF16)
        send(SHARE, sib_out.at[r], sib_in.at[r], sib_recv.at[r], sibling)

    def out_slot(o):
        return o + 7 if o < 0 else o + 6

    def home_far(r):
        arrived(sib_in.at[r], sib_recv.at[r])
        for i, o in enumerate(ROUNDS[r]):
            if o in HAND_ON or (o != 0 and o not in TAKES):
                for h in range(2):
                    span = slice(h * half, (h + 1) * half)
                    dq_out[out_slot(o), span] = (dq[r, h, qslot(o)] + sib_in[r, i, span].astype(F32)).astype(BF16)
                if o not in HAND_ON:
                    send(HOME, dq_out.at[out_slot(o)], dq_in.at[FINAL.index(o)], dq_recv.at[0], at_z(o))
                else:
                    there = HAND_ON[o]
                    j = PAIRS.index(there)
                    send(HOME, dq_out.at[out_slot(o)], pair_in.at[j], pair_recv.at[j], at_z(o - there))

    def home_near(r):
        for i, o in enumerate(ROUNDS[r]):
            if o in TAKES or o == 0:
                if o != 0:
                    j = PAIRS.index(o)
                    arrived(pair_in.at[j], pair_recv.at[j])
                for h in range(2):
                    span = slice(h * half, (h + 1) * half)
                    total = dq[r, h, qslot(o)] + sib_in[r, i, span].astype(F32)
                    if o == 0:
                        dq[r, h, qslot(o)] = total
                    else:
                        dq_out[out_slot(o), span] = (total + pair_in[j, span].astype(F32)).astype(BF16)
                if o != 0:
                    send(HOME, dq_out.at[out_slot(o)], dq_in.at[FINAL.index(o)], dq_recv.at[0], at_z(o))

    def keys_home(h):
        for i, (a, b) in enumerate(PLANE):
            slot = lax.rem(x + a, 4) * 4 + lax.rem(y + b, 4)
            span = pl.ds(pl.multiple_of(slot * half, 16), half)
            kv_out[h, i, 0] = dk[h, span].astype(BF16)
            kv_out[h, i, 1] = dv[h, span].astype(BF16)
            send(KEYS_HOME, kv_out.at[h, i], kv_in.at[h, i], kv_recv.at[h], at_plane(a, b))

    stage(1)

    for i, (used, cp) in enumerate(m_onward):

        @pl.when(used)
        def _():
            arrived(mstage.at[i], ms_recv.at[i])
            cp.start()

    ready(0)
    stage(2)
    ready(1)

    @pl.when(jnp.logical_and(collects, to_self))
    def _():
        arrived(mbuf.at[pl.ds(0, 15)], m_recv.at[0])

    @pl.when(jnp.logical_and(collects, jnp.logical_not(to_self)))
    def _():
        arrived(mbuf, m_recv.at[0])

    mb_copies = [
        pltpu.make_async_remote_copy(
            src_ref=mbuf, dst_ref=mbuf, send_sem=send_sem.at[M_LAST],
            recv_sem=mb_recv.at[0], device_id=at_plane(a, b), device_id_type=MESH,
        )
        for a, b in PLANE
    ]

    @pl.when(collects)
    def _():
        for cp in mb_copies:
            cp.start()

    arrived(kbuf.at[pl.ds(0, 15)], k_recv.at[0])
    late_early(0, True)
    late_early(1, False)
    stage(3)
    ready(2)
    late_early(2, False)

    @pl.when(jnp.logical_not(collects))
    def _():
        arrived(mbuf, mb_recv.at[0])

    sub48 = lax.broadcasted_iota(jnp.int32, (half, 128), 0).astype(F32)
    for slot in range(16):
        start = jnp.broadcast_to(mbuf[slot], (half, 128))
        pk[0, slot * half:(slot + 1) * half] = start + sub48
        pk[1, slot * half:(slot + 1) * half] = top - start + sub48

    early_early(0)
    late_late(0, True)
    share(0)
    early_early(1)
    late_late(1, False)
    share(1)
    home_far(0)
    early_early(2)
    stage(4)
    home_near(0)
    home_far(1)
    ready(3)
    late_early(3, False)
    early_early(3)
    keys_home(0)
    late_late(3, False)
    share(3)
    home_near(1)
    late_late(2, False)
    home_far(3)
    share(2)
    keys_home(1)
    arrived(sib_in.at[2], sib_recv.at[2])
    home_near(2)

    for h in range(2):
        span = pl.ds(pl.multiple_of(my_kslot * half, 16), half)
        rowspan = slice(h * half, (h + 1) * half)
        sk, sv = dk[h, span], dv[h, span]
        arrived(kv_in.at[h], kv_recv.at[h])
        for i in range(15):
            sk = sk + kv_in[h, i, 0].astype(F32)
            sv = sv + kv_in[h, i, 1].astype(F32)
        out_ref[1, rowspan] = sk
        out_ref[2, rowspan] = sv * (1.0 / scale)

    totals = [dq[0, h, my_qslot] for h in range(2)]
    arrived(dq_in, dq_recv.at[0])
    for i in range(len(FINAL)):
        for h in range(2):
            totals[h] = totals[h] + dq_in[i, h * half:(h + 1) * half].astype(F32)
    for h in range(2):
        out_ref[0, h * half:(h + 1) * half] = totals[h]

    sent(CHUNK, qbuf.at[0, pl.ds(0, 7), chunks[0]])
    sent(CHUNK + 1, qbuf.at[0, pl.ds(0, 7), chunks[1]])
    sent(DELIVER, qbuf.at[0])
    sent(SIBLING, qbuf.at[pl.ds(0, 2)])
    sent(KEYS, kbuf.at[pl.ds(0, 15)])
    sent(SHARE, sib_out)
    sent(HOME, dq_out)
    sent(KEYS_HOME, kv_out)

    @pl.when(m_near)
    def _():
        m_direct.wait_send()

    for sign in (1, -1):

        @pl.when(ahead * sign > 4)
        def _():
            m_first[sign].wait_send()

    for used, cp in m_onward:

        @pl.when(used)
        def _():
            cp.wait_send()

    @pl.when(collects)
    def _():
        sent(M_LAST, mwide)


def shards(queries, key_vectors, value_vectors, outputs, out_grad, logsumexp, positions):
    shard, width = queries.shape
    half = shard // 2
    vmem = pl.BlockSpec(memory_space=pltpu.VMEM)
    dma = pltpu.SemaphoreType.DMA
    sums = pl.pallas_call(
        functools.partial(kernel, half),
        name="attention_backward",
        out_shape=jax.ShapeDtypeStruct((3, shard, width), F32),
        in_specs=[pl.BlockSpec(memory_space=pltpu.HBM)] * 7,
        out_specs=vmem,
        scratch_shapes=[
            pltpu.VMEM((4, 8, 2 * shard + 16, width), BF16),
            pltpu.VMEM((16, 2 * shard, width), BF16),
            pltpu.VMEM((shard, width), BF16),
            pltpu.VMEM((1, shard), F32),
            pltpu.VMEM((1, shard), jnp.int32),
            pltpu.VMEM((8, 128), F32),
            pltpu.VMEM((1, 128), F32),
            pltpu.VMEM((4, 1, 128), F32),
            pltpu.VMEM((16, 1, 128), F32),
            pltpu.VMEM((15, 16, 1, 128), F32),
            pltpu.VMEM((2, 16 * half, 128), F32),
            pltpu.VMEM((4, 8, 8 * half), F32),
            pltpu.VMEM((4, 2, 8, half, width), F32),
            pltpu.VMEM((2, 16 * half, width), F32),
            pltpu.VMEM((2, 16 * half, width), F32),
            pltpu.VMEM((4, 4, shard, width), BF16),
            pltpu.VMEM((4, 4, shard, width), BF16),
            pltpu.VMEM((15, shard, width), BF16),
            pltpu.VMEM((len(PAIRS), shard, width), BF16),
            pltpu.VMEM((len(FINAL), shard, width), BF16),
            pltpu.VMEM((2, 15, 2, half, width), BF16),
            pltpu.VMEM((2, 15, 2, half, width), BF16),
            dma((7,)),
            dma((14,)),
            dma((22,)),
            dma((4,)),
            dma((1,)),
            dma((4,)),
            dma((1,)),
            dma((1,)),
            dma((4,)),
            dma((len(PAIRS),)),
            dma((1,)),
            dma((2,)),
        ],
        compiler_params=pltpu.CompilerParams(
            collective_id=0, has_side_effects=True, vmem_limit_bytes=60 * 2 ** 20
        ),
    )(
        queries, key_vectors, value_vectors, outputs, out_grad,
        logsumexp.reshape(1, shard), positions.reshape(1, shard),
    )
    scale = width ** -0.5
    return ((sums[0] * scale).astype(BF16), (sums[1] * scale).astype(BF16), (sums[2] * scale).astype(BF16))


def solution(mesh):
    in_specs = (
        P(("row", "col"), None),
        P(("col", "row"), None),
        P(("col", "row"), None),
        P(("row", "col"), None),
        P(("row", "col"), None),
        P(("row", "col")),
        P(("row", "col")),
    )
    out_specs = (P(("row", "col"), None), P(("col", "row"), None), P(("col", "row"), None))
    return jax.shard_map(shards, mesh=mesh, in_specs=in_specs, out_specs=out_specs, check_vma=False)
```

```python
import functools

import jax
import jax.numpy as jnp
from jax import lax
from jax.experimental import pallas as pl
from jax.experimental.pallas import tpu as pltpu
from jax.sharding import PartitionSpec as P

MESH = pl.DeviceIdType.MESH
F32 = jnp.float32
BF16 = jnp.bfloat16
NT = (((1,), (1,)), ((), ()))
NN = (((1,), (0,)), ((), ()))
TN = (((0,), (0,)), ((), ()))
LOG2E = 1.4426950408889634

ROUNDS = ((0, -1, 1, 2), (-2, 3, -3, 4), (-4, 5, -5, 6), (-6, 7, -7, 8))
ROUND_OF = {o: r for r, offs in enumerate(ROUNDS) for o in offs}
HAND_ON = {8: 6, 7: 5, -7: -5, -6: -4, 4: 3, -3: -2, 2: 1}
TAKES = {b: a for a, b in HAND_ON.items()}
FINAL = tuple(o for offs in ROUNDS for o in offs if o != 0 and o not in HAND_ON)
PLANE = (
    (2, 2), (3, 2), (2, 1), (0, 2), (1, 2), (3, 1), (2, 3), (0, 1), (1, 1), (3, 3), (1, 3), (0, 3), (2, 0), (3, 0), (1, 0),
)
PAIRS = tuple(sorted(HAND_ON[o] for r in (0, 1) for o in ROUNDS[r] if o in HAND_ON))
OUTS = tuple(o for r in (0, 1, 2) for o in ROUNDS[r] if o != 0)
CHUNK, DELIVER, SIBLING, KEYS, SHARE, HOME, KEYS_HOME, M_FIRST, M_LAST, OUTERMOST, M_ONWARD = 0, 2, 3, 4, 5, 6, 7, 8, 9, 10, 11


def q_index(o, c):
    return (o + 7) // 2 if o % 2 else 8 + (o // 2 + (3 if o < 0 else 2)) * 2 + c


def dot(a, b, dims):
    return lax.dot_general(a, b, dims, preferred_element_type=F32)


def device(x, y, z, core):
    return (lax.rem(z, 8) * 4 + x, (y * 2 + z // 8) * 2 + core)


def kernel(
    half, q_hbm, k_hbm, v_hbm, o_hbm, do_hbm, lse_hbm, pos_hbm,
    out_ref,
    qbuf, kbuf, o_ref, lse_ref, pos_ref, rowbuf, mrow, mstage, mbuf, mwide, pk, rows, dq, dk, dv,
    sib_out, sib_in, dq_out, outer_out, pair_in, outer_in, dq_in, kv_out, kv_in,
    in_sem, send_sem, q_recv, qs_recv, k_recv, ms_recv, m_recv, mb_recv, sib_recv, pair_recv, outer_recv, dq_recv, kv_recv,
):
    width = q_hbm.shape[1]
    shard = 2 * half
    scale = width ** -0.5
    row, col = lax.axis_index("row"), lax.axis_index("col")
    z_lo, x = row // 4, lax.rem(row, 4)
    core, z_hi, y = lax.rem(col, 2), lax.rem(col // 2, 2), col // 4
    z = z_hi * 8 + z_lo
    other = 1 - core

    def at_z(o):
        return device(x, y, lax.rem(z + o + 16, 16), core)

    def at_plane(a, b):
        return device(lax.rem(x + a, 4), lax.rem(y + b, 4), z, core)

    sibling = device(x, y, z, other)

    to_z = lax.rem(z, 2) * 8 + lax.rem(x, 2) * 4 + y
    to_core = x // 2
    to_self = jnp.logical_and(to_z == z, to_core == core)
    my_mslot = (z_hi * 2 + core) * 4 + z_lo // 2
    collects = jnp.logical_and(x == core * 2 + z_lo // 4, y == lax.rem(z_lo, 4))

    my_qslot = lax.rem(z, 4) * 2 + core
    my_kslot = x * 4 + y
    inputs = [
        pltpu.make_async_copy(src, dst, in_sem.at[i])
        for i, (src, dst) in enumerate((
            (do_hbm, qbuf.at[0, my_qslot, pl.ds(shard, shard)]),
            (o_hbm, o_ref),
            (lse_hbm, lse_ref),
            (pos_hbm, pos_ref),
            (q_hbm, qbuf.at[0, my_qslot, pl.ds(0, shard)]),
            (k_hbm, kbuf.at[my_kslot, pl.ds(0, shard)]),
            (v_hbm, kbuf.at[my_kslot, pl.ds(shard, shard)]),
        ))
    ]
    for cp in inputs:
        cp.start()

    barrier = pltpu.get_barrier_semaphore()
    greeted = [at_plane(a, b) for a, b in PLANE] + [sibling]
    for o in (-4, -3, -2, -1, 1, 2, 3, 4):
        greeted += [at_z(o), device(x, y, lax.rem(z + o + 16, 16), other)]
    for target in greeted:
        pl.semaphore_signal(barrier, inc=1, device_id=target, device_id_type=MESH)

    def send(kind, src, dst, recv_sem, target):
        pltpu.make_async_remote_copy(
            src_ref=src, dst_ref=dst, send_sem=send_sem.at[kind], recv_sem=recv_sem,
            device_id=target, device_id_type=MESH,
        ).start()

    def sent(kind, whole):
        pltpu.make_async_remote_copy(
            src_ref=whole, dst_ref=whole, send_sem=send_sem.at[kind], recv_sem=mb_recv.at[0],
            device_id=sibling, device_id_type=MESH,
        ).wait_send()

    def arrived(dst, recv_sem):
        pltpu.make_async_remote_copy(
            src_ref=dst, dst_ref=dst, send_sem=send_sem.at[0], recv_sem=recv_sem,
            device_id=sibling, device_id_type=MESH,
        ).wait_recv()

    for cp in inputs:
        cp.wait()
    prod = qbuf[0, my_qslot, shard:2 * shard].astype(F32) * o_ref[...].astype(F32)
    rowbuf[...] = jnp.zeros_like(rowbuf)
    rowbuf[0:1, 0:shard] = lse_ref[...] * LOG2E
    rowbuf[1:2, 0:shard] = jnp.sum(prod.T, axis=0, keepdims=True)
    base = jnp.broadcast_to(pos_ref[0:1, 0:1].astype(F32), (1, 128))
    mrow[...] = base
    shift = lax.rem(my_qslot * half, 128)
    early = pltpu.roll(rowbuf[...], shift, 1)
    late = pltpu.roll(rowbuf[...], lax.rem(shift + 128 - half, 128), 1)
    sub = lax.broadcasted_iota(jnp.int32, (8, 128), 0)
    full = jnp.where(
        sub < 2, early,
        jnp.where(sub < 4, pltpu.roll(late, 2, 0), jnp.where(sub == 4, jnp.broadcast_to(base, (8, 128)), 0.0)),
    )
    hi = full.astype(BF16).astype(F32)
    mid = (full - hi).astype(BF16).astype(F32)
    qbuf[0, my_qslot, 2 * shard:2 * shard + 16] = jnp.concatenate([hi, mid], axis=0).astype(BF16)

    pl.semaphore_wait(barrier, len(greeted))

    def qslot(o):
        return lax.rem(z + o + 16, 4) * 2 + core

    def sslot(o):
        return lax.rem(z + o + 16, 4) * 2 + other

    chunks = (pl.ds(0, shard), pl.ds(shard, shard + 16))

    def directions(o):
        return (1, -1) if o == 0 else ((1,) if o < 0 else (-1,))

    def relay(o, c):
        for sign in directions(o):
            there = o - sign * 2
            if there in ROUND_OF:
                send(
                    CHUNK + c, qbuf.at[ROUND_OF[o], qslot(o), chunks[c]],
                    qbuf.at[ROUND_OF[there], qslot(o), chunks[c]],
                    q_recv.at[q_index(there, c)], at_z(sign * 2),
                )

    def deliver(o):
        for sign in directions(o):
            there = o - sign
            send(
                DELIVER, qbuf.at[ROUND_OF[o], qslot(o)], qbuf.at[ROUND_OF[there], qslot(o)],
                q_recv.at[q_index(there, 1)], at_z(sign),
            )

    def to_sibling(o):
        ref = qbuf.at[ROUND_OF[o], qslot(o)]
        send(SIBLING, ref, ref, qs_recv.at[ROUND_OF[o]], sibling)

    def take(o, c):
        arrived(qbuf.at[ROUND_OF[o], qslot(o), chunks[c]], q_recv.at[q_index(o, c)])

    def take_whole(o):
        arrived(qbuf.at[ROUND_OF[o], qslot(o)], q_recv.at[q_index(o, 1)])

    def keys_out(first, last):
        for i in range(first, last):
            ref = kbuf.at[my_kslot]
            send(KEYS, ref, ref, k_recv.at[0], at_plane(*PLANE[i]))

    relay(0, 0)
    relay(0, 1)
    to_sibling(0)
    deliver(0)
    keys_out(0, 15)

    ahead = lax.rem(to_z - z + 16, 16)
    ahead = jnp.where(ahead > 8, ahead - 16, ahead)

    m_direct = pltpu.make_async_remote_copy(
        src_ref=mrow, dst_ref=mbuf.at[my_mslot], send_sem=send_sem.at[M_FIRST],
        recv_sem=m_recv.at[0], device_id=device(x, y, to_z, to_core), device_id_type=MESH,
    )
    m_first = {
        sign: pltpu.make_async_remote_copy(
            src_ref=mrow, dst_ref=mstage.at[2 * j + core], send_sem=send_sem.at[M_FIRST],
            recv_sem=ms_recv.at[2 * j + core],
            device_id=device(x, y, lax.rem(z + 4 * sign + 16, 16), to_core), device_id_type=MESH,
        )
        for j, sign in enumerate((1, -1))
    }
    m_onward = []
    for j, sign in enumerate((1, -1)):
        for hc in range(2):
            hz = lax.rem(z - 4 * sign + 16, 16)
            far = lax.rem(to_z - hz + 16, 16)
            far = jnp.where(far > 8, far - 16, far)
            mslot = (hz // 8 * 2 + hc) * 4 + lax.rem(hz, 8) // 2
            m_onward.append((
                jnp.logical_and(core == to_core, far * sign > 4),
                pltpu.make_async_remote_copy(
                    src_ref=mstage.at[2 * j + hc], dst_ref=mbuf.at[mslot], send_sem=send_sem.at[M_ONWARD + 2 * j + hc],
                    recv_sem=m_recv.at[0], device_id=device(x, y, to_z, to_core), device_id_type=MESH,
                ),
            ))
    m_near = jnp.logical_and(jnp.logical_not(to_self), jnp.abs(ahead) <= 4)

    @pl.when(m_near)
    def _():
        m_direct.start()

    for sign in (1, -1):

        @pl.when(ahead * sign > 4)
        def _():
            m_first[sign].start()

    @pl.when(to_self)
    def _():
        mbuf[my_mslot] = mrow[...]

    lane = lax.broadcasted_iota(jnp.int32, (8, 128), 1)

    def unpack(r):
        tiles = []
        pieces = []
        for s in range(8):
            raw = qbuf[r, s, 2 * shard:2 * shard + 16].astype(F32)
            pieces.append(raw[0:8] + raw[8:16])
        for j in range(8 * half // 128):
            first, last = 128 * j // half, (128 * j + 127) // half
            tile = pieces[last]
            for s in range(last - 1, first - 1, -1):
                tile = jnp.where(lane < (s + 1) * half - 128 * j, pieces[s], tile)
            tiles.append(tile)
        rows[r] = jnp.concatenate(tiles, axis=1)

    nq = 8 * half
    nk = 8 * half
    lanes = lax.broadcasted_iota(jnp.int32, (1, nq), 1).astype(F32)
    offs = lanes - half * jnp.floor((lanes + 0.5) * (1.0 / half))
    top = 1023.0 * half

    def block(r, kh, qh, kb, masked, first_q, first_k):
        k = kbuf[8 * kb:8 * kb + 8, kh * half:(kh + 1) * half].reshape(nk, width)
        v = kbuf[8 * kb:8 * kb + 8, shard + kh * half:shard + (kh + 1) * half].reshape(nk, width)
        q = qbuf[r, :, qh * half:(qh + 1) * half].reshape(nq, width)
        do = qbuf[r, :, shard + qh * half:shard + (qh + 1) * half].reshape(nq, width)
        lse = rows[r, 2 * qh:2 * qh + 1]
        delta = rows[r, 2 * qh + 1:2 * qh + 2]
        s = dot(k, q, NT)
        dp = dot(v, do, NT)
        p = jnp.exp2(s * (scale * LOG2E) - lse)
        if masked:
            start = rows[r, 4:5]
            pq = (start if qh == 0 else top - start) + offs
            pkk = jnp.concatenate([pk[kh, nk * kb:nk * (kb + 1)]] * (nq // 128), axis=1)
            p = jnp.where(pkk <= pq, p, 0.0)
        ds = (p * (dp - delta)).astype(BF16)
        ph = p.astype(BF16)
        gv, gk, gq = dot(ph, do, NN), dot(ds, q, NN), dot(ds, k, TN)
        span = slice(nk * kb, nk * (kb + 1))
        if first_k:
            dv[kh, span] = gv
            dk[kh, span] = gk
        else:
            dv[kh, span] += gv
            dk[kh, span] += gk
        gq = gq.reshape(8, half, width)
        if first_q:
            dq[r, qh] = gq
        else:
            dq[r, qh] += gq

    def late_early(r, first):
        for kb in range(2):
            block(r, 0, 1, kb, False, kb == 0, first)

    def early_early(r):
        for kb in range(2):
            block(r, 0, 0, kb, True, kb == 0, False)

    def late_late(r, first):
        for kb in range(2):
            block(r, 1, 1, kb, True, False, first)

    def ready(r):
        arrived(qbuf.at[r, pl.ds(0, 4)], qs_recv.at[r])
        unpack(r)

    def nearby(k):
        for o in (-2 * k + 1, 2 * k - 1):
            take_whole(o)
            to_sibling(o)

    def stage(k):
        far = [o for o in (-2 * k, 2 * k) if o in ROUND_OF]
        for c in range(2):
            for o in far:
                take(o, c)
                if k < 4:
                    relay(o, c)
        for o in far:
            if k < 4:
                deliver(o)
            to_sibling(o)
        if k < 4:
            nearby(k)

    def share(r):
        for i, o in enumerate(ROUNDS[r]):
            sib_out[r, i, 0:half] = dq[r, 0, sslot(o)].astype(BF16)
            sib_out[r, i, half:shard] = dq[r, 1, sslot(o)].astype(BF16)
        send(SHARE, sib_out.at[r], sib_in.at[r], sib_recv.at[r], sibling)

    def out_slot(o):
        return OUTS.index(o)

    def home_outermost():
        for i, o in reversed(tuple(enumerate(ROUNDS[3]))):
            j = ROUNDS[2].index(HAND_ON[o])
            nearer = lax.rem(z + o - HAND_ON[o] + 16, 16)
            for n, (slot, to) in enumerate(((qslot(o), core), (sslot(o), other))):
                for h in range(2):
                    outer_out[2 * i + n, h * half:(h + 1) * half] = dq[3, h, slot].astype(BF16)
                send(
                    OUTERMOST, outer_out.at[2 * i + n], outer_in.at[j, n], outer_recv.at[j],
                    device(x, y, nearer, to),
                )

    def home_far(r):
        arrived(sib_in.at[r], sib_recv.at[r])
        for i, o in enumerate(ROUNDS[r]):
            if o in HAND_ON or (o != 0 and o not in TAKES):
                for h in range(2):
                    span = slice(h * half, (h + 1) * half)
                    dq_out[out_slot(o), span] = (dq[r, h, qslot(o)] + sib_in[r, i, span].astype(F32)).astype(BF16)
                if o not in HAND_ON:
                    send(HOME, dq_out.at[out_slot(o)], dq_in.at[FINAL.index(o)], dq_recv.at[0], at_z(o))
                else:
                    there = HAND_ON[o]
                    j = PAIRS.index(there)
                    send(HOME, dq_out.at[out_slot(o)], pair_in.at[j], pair_recv.at[j], at_z(o - there))

    def home_near(r):
        for i, o in reversed(tuple(enumerate(ROUNDS[r]))):
            if o in TAKES or o == 0:
                if o != 0:
                    if r == 2:
                        arrived(outer_in.at[i], outer_recv.at[i])
                    else:
                        j = PAIRS.index(o)
                        arrived(pair_in.at[j], pair_recv.at[j])
                for h in range(2):
                    span = slice(h * half, (h + 1) * half)
                    total = dq[r, h, qslot(o)] + sib_in[r, i, span].astype(F32)
                    if o == 0:
                        dq[r, h, qslot(o)] = total
                    else:
                        if r == 2:
                            more = outer_in[i, 0, span].astype(F32) + outer_in[i, 1, span].astype(F32)
                        else:
                            more = pair_in[j, span].astype(F32)
                        dq_out[out_slot(o), span] = (total + more).astype(BF16)
                if o != 0:
                    send(HOME, dq_out.at[out_slot(o)], dq_in.at[FINAL.index(o)], dq_recv.at[0], at_z(o))

    def keys_home(h):
        for i, (a, b) in enumerate(PLANE):
            slot = lax.rem(x + a, 4) * 4 + lax.rem(y + b, 4)
            span = pl.ds(pl.multiple_of(slot * half, 16), half)
            kv_out[h, i, 0] = dk[h, span].astype(BF16)
            kv_out[h, i, 1] = dv[h, span].astype(BF16)
            send(KEYS_HOME, kv_out.at[h, i], kv_in.at[h, i], kv_recv.at[h], at_plane(a, b))

    stage(1)

    for i, (used, cp) in enumerate(m_onward):

        @pl.when(used)
        def _():
            arrived(mstage.at[i], ms_recv.at[i])
            cp.start()

    ready(0)
    stage(2)
    ready(1)

    @pl.when(jnp.logical_and(collects, to_self))
    def _():
        arrived(mbuf.at[pl.ds(0, 15)], m_recv.at[0])

    @pl.when(jnp.logical_and(collects, jnp.logical_not(to_self)))
    def _():
        arrived(mbuf, m_recv.at[0])

    mb_copies = [
        pltpu.make_async_remote_copy(
            src_ref=mbuf, dst_ref=mbuf, send_sem=send_sem.at[M_LAST],
            recv_sem=mb_recv.at[0], device_id=at_plane(a, b), device_id_type=MESH,
        )
        for a, b in PLANE
    ]

    @pl.when(collects)
    def _():
        for cp in mb_copies:
            cp.start()

    arrived(kbuf.at[pl.ds(0, 15)], k_recv.at[0])
    late_early(0, True)
    late_early(1, False)
    stage(3)
    ready(2)
    late_early(2, False)

    @pl.when(jnp.logical_not(collects))
    def _():
        arrived(mbuf, mb_recv.at[0])

    sub48 = lax.broadcasted_iota(jnp.int32, (half, 128), 0).astype(F32)
    for slot in range(16):
        start = jnp.broadcast_to(mbuf[slot], (half, 128))
        pk[0, slot * half:(slot + 1) * half] = start + sub48
        pk[1, slot * half:(slot + 1) * half] = top - start + sub48

    early_early(0)
    late_late(0, True)
    share(0)
    early_early(1)
    late_late(1, False)
    share(1)
    home_far(0)
    early_early(2)
    nearby(4)
    stage(4)
    home_near(0)
    home_far(1)
    ready(3)
    late_early(3, False)
    early_early(3)
    late_late(3, False)
    home_outermost()
    keys_home(0)
    late_late(2, False)
    share(2)
    keys_home(1)
    home_near(1)
    arrived(sib_in.at[2], sib_recv.at[2])
    home_near(2)

    for h in range(2):
        span = pl.ds(pl.multiple_of(my_kslot * half, 16), half)
        rowspan = slice(h * half, (h + 1) * half)
        sk, sv = dk[h, span], dv[h, span]
        arrived(kv_in.at[h], kv_recv.at[h])
        for i in range(15):
            sk = sk + kv_in[h, i, 0].astype(F32)
            sv = sv + kv_in[h, i, 1].astype(F32)
        out_ref[1, rowspan] = sk
        out_ref[2, rowspan] = sv * (1.0 / scale)

    totals = [dq[0, h, my_qslot] for h in range(2)]
    arrived(dq_in, dq_recv.at[0])
    for i in range(len(FINAL)):
        for h in range(2):
            totals[h] = totals[h] + dq_in[i, h * half:(h + 1) * half].astype(F32)
    for h in range(2):
        out_ref[0, h * half:(h + 1) * half] = totals[h]

    sent(CHUNK, qbuf.at[0, pl.ds(0, 7), chunks[0]])
    sent(CHUNK + 1, qbuf.at[0, pl.ds(0, 7), chunks[1]])
    sent(DELIVER, qbuf.at[0])
    sent(SIBLING, qbuf.at[pl.ds(0, 2)])
    sent(KEYS, kbuf.at[pl.ds(0, 15)])
    sent(SHARE, sib_out)
    sent(HOME, dq_out)
    sent(OUTERMOST, outer_out)
    sent(KEYS_HOME, kv_out)

    @pl.when(m_near)
    def _():
        m_direct.wait_send()

    for sign in (1, -1):

        @pl.when(ahead * sign > 4)
        def _():
            m_first[sign].wait_send()

    for used, cp in m_onward:

        @pl.when(used)
        def _():
            cp.wait_send()

    @pl.when(collects)
    def _():
        sent(M_LAST, mwide)


def shards(queries, key_vectors, value_vectors, outputs, out_grad, logsumexp, positions):
    shard, width = queries.shape
    half = shard // 2
    vmem = pl.BlockSpec(memory_space=pltpu.VMEM)
    dma = pltpu.SemaphoreType.DMA
    sums = pl.pallas_call(
        functools.partial(kernel, half),
        name="attention_backward",
        out_shape=pltpu.VMEM((3, shard, width), F32),
        in_specs=[pl.BlockSpec(memory_space=pltpu.HBM)] * 7,
        out_specs=vmem,
        scratch_shapes=[
            pltpu.VMEM((4, 8, 2 * shard + 16, width), BF16),
            pltpu.VMEM((16, 2 * shard, width), BF16),
            pltpu.VMEM((shard, width), BF16),
            pltpu.VMEM((1, shard), F32),
            pltpu.VMEM((1, shard), jnp.int32),
            pltpu.VMEM((8, 128), F32),
            pltpu.VMEM((1, 128), F32),
            pltpu.VMEM((4, 1, 128), F32),
            pltpu.VMEM((16, 1, 128), F32),
            pltpu.VMEM((15, 16, 1, 128), F32),
            pltpu.VMEM((2, 16 * half, 128), F32),
            pltpu.VMEM((4, 8, 8 * half), F32),
            pltpu.VMEM((4, 2, 8, half, width), F32),
            pltpu.VMEM((2, 16 * half, width), F32),
            pltpu.VMEM((2, 16 * half, width), F32),
            pltpu.VMEM((3, 4, shard, width), BF16),
            pltpu.VMEM((3, 4, shard, width), BF16),
            pltpu.VMEM((len(OUTS), shard, width), BF16),
            pltpu.VMEM((8, shard, width), BF16),
            pltpu.VMEM((len(PAIRS), shard, width), BF16),
            pltpu.VMEM((4, 2, shard, width), BF16),
            pltpu.VMEM((len(FINAL), shard, width), BF16),
            pltpu.VMEM((2, 15, 2, half, width), BF16),
            pltpu.VMEM((2, 15, 2, half, width), BF16),
            dma((7,)),
            dma((15,)),
            dma((22,)),
            dma((4,)),
            dma((1,)),
            dma((4,)),
            dma((1,)),
            dma((1,)),
            dma((3,)),
            dma((len(PAIRS),)),
            dma((4,)),
            dma((1,)),
            dma((2,)),
        ],
        compiler_params=pltpu.CompilerParams(
            collective_id=0, has_side_effects=True, vmem_limit_bytes=60 * 2 ** 20
        ),
    )(
        queries, key_vectors, value_vectors, outputs, out_grad,
        logsumexp.reshape(1, shard), positions.reshape(1, shard),
    )
    scale = width ** -0.5
    return ((sums[0] * scale).astype(BF16), (sums[1] * scale).astype(BF16), (sums[2] * scale).astype(BF16))


def solution(mesh):
    in_specs = (
        P(("row", "col"), None),
        P(("col", "row"), None),
        P(("col", "row"), None),
        P(("row", "col"), None),
        P(("row", "col"), None),
        P(("row", "col")),
        P(("row", "col")),
    )
    out_specs = (P(("row", "col"), None), P(("col", "row"), None), P(("col", "row"), None))
    return jax.shard_map(shards, mesh=mesh, in_specs=in_specs, out_specs=out_specs, check_vma=False)
```

```python
import functools

import jax
import jax.numpy as jnp
from jax import lax
from jax.experimental import pallas as pl
from jax.experimental.pallas import tpu as pltpu
from jax.sharding import PartitionSpec as P

MESH = pl.DeviceIdType.MESH
F32 = jnp.float32
BF16 = jnp.bfloat16
NT = (((1,), (1,)), ((), ()))
NN = (((1,), (0,)), ((), ()))
TN = (((0,), (0,)), ((), ()))
LOG2E = 1.4426950408889634

ROUNDS = ((0, -1, 1, 2), (-2, 3, -3, 4), (-4, 5, -5, 6), (-6, 7, -7, 8))
ROUND_OF = {o: r for r, offs in enumerate(ROUNDS) for o in offs}
HAND_ON = {8: 6, 7: 5, -7: -5, -6: -4, 4: 3, -3: -2, 2: 1}
TAKES = {b: a for a, b in HAND_ON.items()}
FINAL = tuple(o for offs in ROUNDS for o in offs if o != 0 and o not in HAND_ON)
PLANE = (
    (2, 2), (3, 2), (2, 1), (0, 2), (1, 2), (3, 1), (2, 3), (0, 1), (1, 1), (3, 3), (1, 3), (0, 3), (2, 0), (3, 0), (1, 0),
)
PAIRS = tuple(sorted(HAND_ON[o] for r in (0, 1) for o in ROUNDS[r] if o in HAND_ON))
OUTS = tuple(o for r in (0, 1, 2) for o in ROUNDS[r] if o != 0)
CUTS = (0, 64, 128, 208)
CHUNKS = len(CUTS) - 1
DELIVER, SIBLING, KEYS, SHARE, HOME, KEYS_HOME, M_FIRST, M_LAST, OUTERMOST, M_ONWARD, CHUNK = 0, 1, 2, 3, 4, 5, 6, 7, 8, 9, 13


def q_index(o, c):
    return (o + 7) // 2 if o % 2 else 8 + (o // 2 + (3 if o < 0 else 2)) * CHUNKS + c


def dot(a, b, dims):
    return lax.dot_general(a, b, dims, preferred_element_type=F32)


def device(x, y, z, core):
    return (lax.rem(z, 8) * 4 + x, (y * 2 + z // 8) * 2 + core)


def kernel(
    half, q_hbm, k_hbm, v_hbm, o_hbm, do_hbm, lse_hbm, pos_hbm,
    out_ref,
    qbuf, kbuf, o_ref, lse_ref, pos_ref, rowbuf, mrow, mstage, mbuf, mwide, pk, rows, dq, dk, dv,
    sib_out, sib_in, dq_out, outer_out, pair_in, outer_in, dq_in, kv_out, kv_in,
    in_sem, send_sem, q_recv, qs_recv, k_recv, ms_recv, m_recv, mb_recv, sib_recv, pair_recv, outer_recv, dq_recv, kv_recv,
):
    width = q_hbm.shape[1]
    shard = 2 * half
    scale = width ** -0.5
    row, col = lax.axis_index("row"), lax.axis_index("col")
    z_lo, x = row // 4, lax.rem(row, 4)
    core, z_hi, y = lax.rem(col, 2), lax.rem(col // 2, 2), col // 4
    z = z_hi * 8 + z_lo
    other = 1 - core

    def at_z(o):
        return device(x, y, lax.rem(z + o + 16, 16), core)

    def at_plane(a, b):
        return device(lax.rem(x + a, 4), lax.rem(y + b, 4), z, core)

    sibling = device(x, y, z, other)

    to_z = lax.rem(z, 2) * 8 + lax.rem(x, 2) * 4 + y
    to_core = x // 2
    to_self = jnp.logical_and(to_z == z, to_core == core)
    my_mslot = (z_hi * 2 + core) * 4 + z_lo // 2
    collects = jnp.logical_and(x == core * 2 + z_lo // 4, y == lax.rem(z_lo, 4))

    my_qslot = lax.rem(z, 4) * 2 + core
    my_kslot = x * 4 + y
    inputs = [
        pltpu.make_async_copy(src, dst, in_sem.at[i])
        for i, (src, dst) in enumerate((
            (do_hbm, qbuf.at[0, my_qslot, pl.ds(shard, shard)]),
            (o_hbm, o_ref),
            (lse_hbm, lse_ref),
            (pos_hbm, pos_ref),
            (q_hbm, qbuf.at[0, my_qslot, pl.ds(0, shard)]),
            (k_hbm, kbuf.at[my_kslot, pl.ds(0, shard)]),
            (v_hbm, kbuf.at[my_kslot, pl.ds(shard, shard)]),
        ))
    ]
    for cp in inputs:
        cp.start()

    barrier = pltpu.get_barrier_semaphore()
    greeted = [at_plane(a, b) for a, b in PLANE] + [sibling]
    for o in (-4, -3, -2, -1, 1, 2, 3, 4):
        greeted += [at_z(o), device(x, y, lax.rem(z + o + 16, 16), other)]
    for target in greeted:
        pl.semaphore_signal(barrier, inc=1, device_id=target, device_id_type=MESH)

    def send(kind, src, dst, recv_sem, target):
        pltpu.make_async_remote_copy(
            src_ref=src, dst_ref=dst, send_sem=send_sem.at[kind], recv_sem=recv_sem,
            device_id=target, device_id_type=MESH,
        ).start()

    def sent(kind, whole):
        pltpu.make_async_remote_copy(
            src_ref=whole, dst_ref=whole, send_sem=send_sem.at[kind], recv_sem=mb_recv.at[0],
            device_id=sibling, device_id_type=MESH,
        ).wait_send()

    def arrived(dst, recv_sem):
        pltpu.make_async_remote_copy(
            src_ref=dst, dst_ref=dst, send_sem=send_sem.at[0], recv_sem=recv_sem,
            device_id=sibling, device_id_type=MESH,
        ).wait_recv()

    for cp in inputs:
        cp.wait()
    prod = qbuf[0, my_qslot, shard:2 * shard].astype(F32) * o_ref[...].astype(F32)
    rowbuf[...] = jnp.zeros_like(rowbuf)
    rowbuf[0:1, 0:shard] = lse_ref[...] * LOG2E
    rowbuf[1:2, 0:shard] = jnp.sum(prod.T, axis=0, keepdims=True)
    base = jnp.broadcast_to(pos_ref[0:1, 0:1].astype(F32), (1, 128))
    mrow[...] = base
    shift = lax.rem(my_qslot * half, 128)
    early = pltpu.roll(rowbuf[...], shift, 1)
    late = pltpu.roll(rowbuf[...], lax.rem(shift + 128 - half, 128), 1)
    sub = lax.broadcasted_iota(jnp.int32, (8, 128), 0)
    full = jnp.where(
        sub < 2, early,
        jnp.where(sub < 4, pltpu.roll(late, 2, 0), jnp.where(sub == 4, jnp.broadcast_to(base, (8, 128)), 0.0)),
    )
    hi = full.astype(BF16).astype(F32)
    mid = (full - hi).astype(BF16).astype(F32)
    qbuf[0, my_qslot, 2 * shard:2 * shard + 16] = jnp.concatenate([hi, mid], axis=0).astype(BF16)

    pl.semaphore_wait(barrier, len(greeted))

    def qslot(o):
        return lax.rem(z + o + 16, 4) * 2 + core

    def sslot(o):
        return lax.rem(z + o + 16, 4) * 2 + other

    chunks = tuple(pl.ds(a, b - a) for a, b in zip(CUTS, CUTS[1:]))

    def directions(o):
        return (1, -1) if o == 0 else ((1,) if o < 0 else (-1,))

    def relay(o, c):
        for sign in directions(o):
            there = o - sign * 2
            if there in ROUND_OF:
                send(
                    CHUNK + c, qbuf.at[ROUND_OF[o], qslot(o), chunks[c]],
                    qbuf.at[ROUND_OF[there], qslot(o), chunks[c]],
                    q_recv.at[q_index(there, c)], at_z(sign * 2),
                )

    def deliver(o):
        for sign in directions(o):
            there = o - sign
            send(
                DELIVER, qbuf.at[ROUND_OF[o], qslot(o)], qbuf.at[ROUND_OF[there], qslot(o)],
                q_recv.at[q_index(there, 1)], at_z(sign),
            )

    def to_sibling(o):
        ref = qbuf.at[ROUND_OF[o], qslot(o)]
        send(SIBLING, ref, ref, qs_recv.at[ROUND_OF[o]], sibling)

    def take(o, c):
        arrived(qbuf.at[ROUND_OF[o], qslot(o), chunks[c]], q_recv.at[q_index(o, c)])

    def take_whole(o):
        arrived(qbuf.at[ROUND_OF[o], qslot(o)], q_recv.at[q_index(o, 1)])

    def keys_out(first, last):
        for i in range(first, last):
            ref = kbuf.at[my_kslot]
            send(KEYS, ref, ref, k_recv.at[0], at_plane(*PLANE[i]))

    for c in range(CHUNKS):
        relay(0, c)
    to_sibling(0)
    deliver(0)
    keys_out(0, 15)

    ahead = lax.rem(to_z - z + 16, 16)
    ahead = jnp.where(ahead > 8, ahead - 16, ahead)

    m_direct = pltpu.make_async_remote_copy(
        src_ref=mrow, dst_ref=mbuf.at[my_mslot], send_sem=send_sem.at[M_FIRST],
        recv_sem=m_recv.at[0], device_id=device(x, y, to_z, to_core), device_id_type=MESH,
    )
    m_first = {
        sign: pltpu.make_async_remote_copy(
            src_ref=mrow, dst_ref=mstage.at[2 * j + core], send_sem=send_sem.at[M_FIRST],
            recv_sem=ms_recv.at[2 * j + core],
            device_id=device(x, y, lax.rem(z + 4 * sign + 16, 16), to_core), device_id_type=MESH,
        )
        for j, sign in enumerate((1, -1))
    }
    m_onward = []
    for j, sign in enumerate((1, -1)):
        for hc in range(2):
            hz = lax.rem(z - 4 * sign + 16, 16)
            far = lax.rem(to_z - hz + 16, 16)
            far = jnp.where(far > 8, far - 16, far)
            mslot = (hz // 8 * 2 + hc) * 4 + lax.rem(hz, 8) // 2
            m_onward.append((
                jnp.logical_and(core == to_core, far * sign > 4),
                pltpu.make_async_remote_copy(
                    src_ref=mstage.at[2 * j + hc], dst_ref=mbuf.at[mslot], send_sem=send_sem.at[M_ONWARD + 2 * j + hc],
                    recv_sem=m_recv.at[0], device_id=device(x, y, to_z, to_core), device_id_type=MESH,
                ),
            ))
    m_near = jnp.logical_and(jnp.logical_not(to_self), jnp.abs(ahead) <= 4)

    @pl.when(m_near)
    def _():
        m_direct.start()

    for sign in (1, -1):

        @pl.when(ahead * sign > 4)
        def _():
            m_first[sign].start()

    @pl.when(to_self)
    def _():
        mbuf[my_mslot] = mrow[...]

    lane = lax.broadcasted_iota(jnp.int32, (8, 128), 1)

    def unpack(r):
        tiles = []
        pieces = []
        for s in range(8):
            raw = qbuf[r, s, 2 * shard:2 * shard + 16].astype(F32)
            pieces.append(raw[0:8] + raw[8:16])
        for j in range(8 * half // 128):
            first, last = 128 * j // half, (128 * j + 127) // half
            tile = pieces[last]
            for s in range(last - 1, first - 1, -1):
                tile = jnp.where(lane < (s + 1) * half - 128 * j, pieces[s], tile)
            tiles.append(tile)
        rows[r] = jnp.concatenate(tiles, axis=1)

    nq = 8 * half
    nk = 8 * half
    lanes = lax.broadcasted_iota(jnp.int32, (1, nq), 1).astype(F32)
    offs = lanes - half * jnp.floor((lanes + 0.5) * (1.0 / half))
    top = 1023.0 * half

    def block(r, kh, qh, kb, masked, first_q, first_k):
        k = kbuf[8 * kb:8 * kb + 8, kh * half:(kh + 1) * half].reshape(nk, width)
        v = kbuf[8 * kb:8 * kb + 8, shard + kh * half:shard + (kh + 1) * half].reshape(nk, width)
        q = qbuf[r, :, qh * half:(qh + 1) * half].reshape(nq, width)
        do = qbuf[r, :, shard + qh * half:shard + (qh + 1) * half].reshape(nq, width)
        lse = rows[r, 2 * qh:2 * qh + 1]
        delta = rows[r, 2 * qh + 1:2 * qh + 2]
        s = dot(k, q, NT)
        dp = dot(v, do, NT)
        p = jnp.exp2(s * (scale * LOG2E) - lse)
        if masked:
            start = rows[r, 4:5]
            pq = (start if qh == 0 else top - start) + offs
            pkk = jnp.concatenate([pk[kh, nk * kb:nk * (kb + 1)]] * (nq // 128), axis=1)
            p = jnp.where(pkk <= pq, p, 0.0)
        ds = (p * (dp - delta)).astype(BF16)
        ph = p.astype(BF16)
        gv, gk, gq = dot(ph, do, NN), dot(ds, q, NN), dot(ds, k, TN)
        span = slice(nk * kb, nk * (kb + 1))
        if first_k:
            dv[kh, span] = gv
            dk[kh, span] = gk
        else:
            dv[kh, span] += gv
            dk[kh, span] += gk
        gq = gq.reshape(8, half, width)
        if first_q:
            dq[r, qh] = gq
        else:
            dq[r, qh] += gq

    def late_early(r, first):
        for kb in range(2):
            block(r, 0, 1, kb, False, kb == 0, first)

    def early_early(r):
        for kb in range(2):
            block(r, 0, 0, kb, True, kb == 0, False)

    def late_late(r, first):
        for kb in range(2):
            block(r, 1, 1, kb, True, False, first)

    def ready(r):
        arrived(qbuf.at[r, pl.ds(0, 4)], qs_recv.at[r])
        unpack(r)

    def nearby(k):
        for o in (-2 * k + 1, 2 * k - 1):
            take_whole(o)
            to_sibling(o)

    def stage(k):
        far = [o for o in (-2 * k, 2 * k) if o in ROUND_OF]
        for c in range(CHUNKS):
            for o in far:
                take(o, c)
                if k < 4:
                    relay(o, c)
        for o in far:
            if k < 4:
                deliver(o)
            to_sibling(o)
        if k < 4:
            nearby(k)

    def share(r):
        for i, o in enumerate(ROUNDS[r]):
            sib_out[r, i, 0:half] = dq[r, 0, sslot(o)].astype(BF16)
            sib_out[r, i, half:shard] = dq[r, 1, sslot(o)].astype(BF16)
        send(SHARE, sib_out.at[r], sib_in.at[r], sib_recv.at[r], sibling)

    def out_slot(o):
        return OUTS.index(o)

    def home_outermost():
        for i, o in reversed(tuple(enumerate(ROUNDS[3]))):
            j = ROUNDS[2].index(HAND_ON[o])
            nearer = lax.rem(z + o - HAND_ON[o] + 16, 16)
            for n, (slot, to) in enumerate(((qslot(o), core), (sslot(o), other))):
                for h in range(2):
                    outer_out[2 * i + n, h * half:(h + 1) * half] = dq[3, h, slot].astype(BF16)
                send(
                    OUTERMOST, outer_out.at[2 * i + n], outer_in.at[j, n], outer_recv.at[j],
                    device(x, y, nearer, to),
                )

    def home_far(r):
        arrived(sib_in.at[r], sib_recv.at[r])
        for i, o in enumerate(ROUNDS[r]):
            if o in HAND_ON or (o != 0 and o not in TAKES):
                for h in range(2):
                    span = slice(h * half, (h + 1) * half)
                    dq_out[out_slot(o), span] = (dq[r, h, qslot(o)] + sib_in[r, i, span].astype(F32)).astype(BF16)
                if o not in HAND_ON:
                    send(HOME, dq_out.at[out_slot(o)], dq_in.at[FINAL.index(o)], dq_recv.at[0], at_z(o))
                else:
                    there = HAND_ON[o]
                    j = PAIRS.index(there)
                    send(HOME, dq_out.at[out_slot(o)], pair_in.at[j], pair_recv.at[j], at_z(o - there))

    def home_near(r):
        for i, o in reversed(tuple(enumerate(ROUNDS[r]))):
            if o in TAKES or o == 0:
                if o != 0:
                    if r == 2:
                        arrived(outer_in.at[i], outer_recv.at[i])
                    else:
                        j = PAIRS.index(o)
                        arrived(pair_in.at[j], pair_recv.at[j])
                for h in range(2):
                    span = slice(h * half, (h + 1) * half)
                    total = dq[r, h, qslot(o)] + sib_in[r, i, span].astype(F32)
                    if o == 0:
                        dq[r, h, qslot(o)] = total
                    else:
                        if r == 2:
                            more = outer_in[i, 0, span].astype(F32) + outer_in[i, 1, span].astype(F32)
                        else:
                            more = pair_in[j, span].astype(F32)
                        dq_out[out_slot(o), span] = (total + more).astype(BF16)
                if o != 0:
                    send(HOME, dq_out.at[out_slot(o)], dq_in.at[FINAL.index(o)], dq_recv.at[0], at_z(o))

    def keys_home(h):
        for i, (a, b) in enumerate(PLANE):
            slot = lax.rem(x + a, 4) * 4 + lax.rem(y + b, 4)
            span = pl.ds(pl.multiple_of(slot * half, 16), half)
            kv_out[h, i, 0] = dk[h, span].astype(BF16)
            kv_out[h, i, 1] = dv[h, span].astype(BF16)
            send(KEYS_HOME, kv_out.at[h, i], kv_in.at[h, i], kv_recv.at[h], at_plane(a, b))

    stage(1)

    for i, (used, cp) in enumerate(m_onward):

        @pl.when(used)
        def _():
            arrived(mstage.at[i], ms_recv.at[i])
            cp.start()

    ready(0)
    stage(2)
    ready(1)

    @pl.when(jnp.logical_and(collects, to_self))
    def _():
        arrived(mbuf.at[pl.ds(0, 15)], m_recv.at[0])

    @pl.when(jnp.logical_and(collects, jnp.logical_not(to_self)))
    def _():
        arrived(mbuf, m_recv.at[0])

    mb_copies = [
        pltpu.make_async_remote_copy(
            src_ref=mbuf, dst_ref=mbuf, send_sem=send_sem.at[M_LAST],
            recv_sem=mb_recv.at[0], device_id=at_plane(a, b), device_id_type=MESH,
        )
        for a, b in PLANE
    ]

    @pl.when(collects)
    def _():
        for cp in mb_copies:
            cp.start()

    arrived(kbuf.at[pl.ds(0, 15)], k_recv.at[0])
    late_early(0, True)
    late_early(1, False)
    stage(3)
    ready(2)
    late_early(2, False)

    @pl.when(jnp.logical_not(collects))
    def _():
        arrived(mbuf, mb_recv.at[0])

    sub48 = lax.broadcasted_iota(jnp.int32, (half, 128), 0).astype(F32)
    for slot in range(16):
        start = jnp.broadcast_to(mbuf[slot], (half, 128))
        pk[0, slot * half:(slot + 1) * half] = start + sub48
        pk[1, slot * half:(slot + 1) * half] = top - start + sub48

    early_early(0)
    late_late(0, True)
    share(0)
    early_early(1)
    late_late(1, False)
    share(1)
    home_far(0)
    early_early(2)
    nearby(4)
    stage(4)
    home_near(0)
    home_far(1)
    ready(3)
    late_early(3, False)
    early_early(3)
    late_late(3, False)
    home_outermost()
    keys_home(0)
    late_late(2, False)
    share(2)
    keys_home(1)
    home_near(1)
    arrived(sib_in.at[2], sib_recv.at[2])
    home_near(2)

    for h in range(2):
        span = pl.ds(pl.multiple_of(my_kslot * half, 16), half)
        rowspan = slice(h * half, (h + 1) * half)
        sk, sv = dk[h, span], dv[h, span]
        arrived(kv_in.at[h], kv_recv.at[h])
        for i in range(15):
            sk = sk + kv_in[h, i, 0].astype(F32)
            sv = sv + kv_in[h, i, 1].astype(F32)
        out_ref[1, rowspan] = sk
        out_ref[2, rowspan] = sv * (1.0 / scale)

    totals = [dq[0, h, my_qslot] for h in range(2)]
    arrived(dq_in, dq_recv.at[0])
    for i in range(len(FINAL)):
        for h in range(2):
            totals[h] = totals[h] + dq_in[i, h * half:(h + 1) * half].astype(F32)
    for h in range(2):
        out_ref[0, h * half:(h + 1) * half] = totals[h]

    for c in range(CHUNKS):
        sent(CHUNK + c, qbuf.at[0, pl.ds(0, 7), chunks[c]])
    sent(DELIVER, qbuf.at[0])
    sent(SIBLING, qbuf.at[pl.ds(0, 2)])
    sent(KEYS, kbuf.at[pl.ds(0, 15)])
    sent(SHARE, sib_out)
    sent(HOME, dq_out)
    sent(OUTERMOST, outer_out)
    sent(KEYS_HOME, kv_out)

    @pl.when(m_near)
    def _():
        m_direct.wait_send()

    for sign in (1, -1):

        @pl.when(ahead * sign > 4)
        def _():
            m_first[sign].wait_send()

    for used, cp in m_onward:

        @pl.when(used)
        def _():
            cp.wait_send()

    @pl.when(collects)
    def _():
        sent(M_LAST, mwide)


def shards(queries, key_vectors, value_vectors, outputs, out_grad, logsumexp, positions):
    shard, width = queries.shape
    half = shard // 2
    vmem = pl.BlockSpec(memory_space=pltpu.VMEM)
    dma = pltpu.SemaphoreType.DMA
    sums = pl.pallas_call(
        functools.partial(kernel, half),
        name="attention_backward",
        out_shape=pltpu.VMEM((3, shard, width), F32),
        in_specs=[pl.BlockSpec(memory_space=pltpu.HBM)] * 7,
        out_specs=vmem,
        scratch_shapes=[
            pltpu.VMEM((4, 8, 2 * shard + 16, width), BF16),
            pltpu.VMEM((16, 2 * shard, width), BF16),
            pltpu.VMEM((shard, width), BF16),
            pltpu.VMEM((1, shard), F32),
            pltpu.VMEM((1, shard), jnp.int32),
            pltpu.VMEM((8, 128), F32),
            pltpu.VMEM((1, 128), F32),
            pltpu.VMEM((4, 1, 128), F32),
            pltpu.VMEM((16, 1, 128), F32),
            pltpu.VMEM((15, 16, 1, 128), F32),
            pltpu.VMEM((2, 16 * half, 128), F32),
            pltpu.VMEM((4, 8, 8 * half), F32),
            pltpu.VMEM((4, 2, 8, half, width), F32),
            pltpu.VMEM((2, 16 * half, width), F32),
            pltpu.VMEM((2, 16 * half, width), F32),
            pltpu.VMEM((3, 4, shard, width), BF16),
            pltpu.VMEM((3, 4, shard, width), BF16),
            pltpu.VMEM((len(OUTS), shard, width), BF16),
            pltpu.VMEM((8, shard, width), BF16),
            pltpu.VMEM((len(PAIRS), shard, width), BF16),
            pltpu.VMEM((4, 2, shard, width), BF16),
            pltpu.VMEM((len(FINAL), shard, width), BF16),
            pltpu.VMEM((2, 15, 2, half, width), BF16),
            pltpu.VMEM((2, 15, 2, half, width), BF16),
            dma((7,)),
            dma((CHUNK + CHUNKS,)),
            dma((8 + 7 * CHUNKS,)),
            dma((4,)),
            dma((1,)),
            dma((4,)),
            dma((1,)),
            dma((1,)),
            dma((3,)),
            dma((len(PAIRS),)),
            dma((4,)),
            dma((1,)),
            dma((2,)),
        ],
        compiler_params=pltpu.CompilerParams(
            collective_id=0, has_side_effects=True, vmem_limit_bytes=60 * 2 ** 20
        ),
    )(
        queries, key_vectors, value_vectors, outputs, out_grad,
        logsumexp.reshape(1, shard), positions.reshape(1, shard),
    )
    scale = width ** -0.5
    return ((sums[0] * scale).astype(BF16), (sums[1] * scale).astype(BF16), (sums[2] * scale).astype(BF16))


def solution(mesh):
    in_specs = (
        P(("row", "col"), None),
        P(("col", "row"), None),
        P(("col", "row"), None),
        P(("row", "col"), None),
        P(("row", "col"), None),
        P(("row", "col")),
        P(("row", "col")),
    )
    out_specs = (P(("row", "col"), None), P(("col", "row"), None), P(("col", "row"), None))
    return jax.shard_map(shards, mesh=mesh, in_specs=in_specs, out_specs=out_specs, check_vma=False)
```
